32 devices in a mesh: tm: 4 (over z), gx: 4 (over x, core), gy: 2 (over y).
Axes of the slice: x: 2, y: 2, z: 4, core: 2. Of those that a mesh axis runs over, the one named last changes fastest.
Arguments:
- lagrange: float32 [8, 8, 256, 256], P('tm', None, 'gx', 'gy'), may hold values from -6 to 6
- obs_lagrange: float32 [8, 4, 2, 1024], P('tm', 'gx', 'gy'), may hold values from -6 to 6
- increment: float32 [8, 8, 256, 256], P('tm', None, 'gx', 'gy'), may hold values from -6 to 6
- forcing: float32 [8, 8, 256, 256], P('tm', None, 'gx', 'gy'), may hold values from -6 to 6
- departures: float32 [8, 4, 2, 1024], P('tm', 'gx', 'gy'), may hold values from -6 to 6
- model_var: float32 [8, 8, 256, 256], P('tm', None, 'gx', 'gy'), may hold values from 0.3 to 3
- obs_var: float32 [8, 4, 2, 1024], P('tm', 'gx', 'gy'), may hold values from 0.5 to 2
- wind_east: float32 [8, 8, 256, 256], P('tm', None, 'gx', 'gy'), may hold values from -0.3 to 0.3
- wind_north: float32 [8, 8, 256, 256], P('tm', None, 'gx', 'gy'), may hold values from -0.3 to 0.3
- obs_cells: int32 [8, 4, 2, 1024], P('tm', 'gx', 'gy'), may hold values from 0 to 65535
- step_count: int32 [8], P('tm'), may hold values from 1 to 4, as said below
Outputs:
- lagrange_next: float32 [8, 8, 256, 256], P('tm', None, 'gx', 'gy')
- obs_lagrange_next: float32 [8, 4, 2, 1024], P('tm', 'gx', 'gy')
- increment_next: float32 [8, 8, 256, 256], P('tm', None, 'gx', 'gy')
- residual_model: float32 [8, 8, 256, 256], P('tm', None, 'gx', 'gy')
- residual_obs: float32 [8, 4, 2, 1024], P('tm', 'gx', 'gy')
- residual_increment: float32 [8, 8, 256, 256], P('tm', None, 'gx', 'gy')
The draws below stay inside these ranges and needn't reach their ends.
Inputs may be any that keep to these rules, and one draw needn't show every extreme that they name: `step_count`: each sub-window's number of model steps; at least one sub-window takes 4.
All inputs are finite; a program needn't handle non-finite values.
Results may differ from the reference program's by a relative error of at most 0.0003.
Values sent between devices are 32-bit elements; how exact they have to be, the bound alone decides.
A program may use at most 64 MiB of HBM per device.

```python
import math
import jax
import jax.numpy as jnp
from jax import lax

CX = 64
CY = 128
LEV = 8
MAXSTEP = 4
NOBS = 1024
NSUB = 8
NX = 256
NY = 256
N_GX = 4
N_GY = 2


def draw_step_count(key, part):
    key = jax.random.fold_in(key, 11)
    counts = jax.random.randint(key, (NSUB,), 1, MAXSTEP + 1, dtype=jnp.int32)
    where_full = jax.random.randint(jax.random.fold_in(key, 12), (), 0, NSUB, dtype=jnp.int32)
    return counts.at[where_full].set(MAXSTEP)


def set_ends(drawn, rng, least, largest):
    index_at = [jax.random.randint(jax.random.fold_in(rng, axis), (), 0, length) for axis, length in enumerate(drawn.shape)]
    longest = drawn.shape.index(max(drawn.shape))
    neighbour = index_at[:longest] + [(index_at[longest] + 1) % drawn.shape[longest]] + index_at[longest + 1:]
    return drawn.at[tuple(index_at)].set(least).at[tuple(neighbour)].set(largest)


def block_levels(own_key, dims, pieces, low, high):
    factor_of, own = 1.0, jax.random.fold_in(own_key, 6)
    for axis_at, shards_of in pieces:
        steps = jnp.exp(jax.random.uniform(jax.random.fold_in(own, axis_at), (shards_of,), jnp.float32, low / len(pieces), high / len(pieces)))
        factor_of = factor_of * jnp.repeat(steps, dims[axis_at] // shards_of).reshape([-1 if axis == axis_at else 1 for axis in range(len(dims))])
    return factor_of


def gaussian(rng, dims, scale, bound, cuts=(), kind=jnp.bfloat16):
    result = jax.random.normal(rng, dims, jnp.float32) * scale
    if len(cuts) > 0:
        result = block_levels(rng, dims, cuts, -0.22, 0.18) * result
    return jnp.clip(result, min=-bound, max=bound).astype(kind)


def setup_inputs(seed: int = 0) -> dict:
    splits = jax.random.split(jax.random.key(seed), 12)
    lagrange = gaussian(splits[0], (NSUB, LEV, NX, NY), 1.0, 6.0, ((0, 4), (2, 4), (3, 2)), jnp.float32)
    obs_lagrange = gaussian(splits[1], (NSUB, N_GX, N_GY, NOBS), 1.0, 6.0, ((0, 4), (1, 4), (2, 2)), jnp.float32)
    increment = gaussian(splits[2], (NSUB, LEV, NX, NY), 1.0, 6.0, ((0, 4), (2, 4), (3, 2)), jnp.float32)
    forcing = gaussian(splits[3], (NSUB, LEV, NX, NY), 1.0, 6.0, ((0, 4), (2, 4), (3, 2)), jnp.float32)
    departures = gaussian(splits[4], (NSUB, N_GX, N_GY, NOBS), 1.0, 6.0, ((0, 4), (1, 4), (2, 2)), jnp.float32)
    model_var = jnp.clip(jnp.exp(math.log(3.0) - 2.3025851 * jax.random.uniform(splits[5], (NSUB, LEV, NX, NY), jnp.float32) ** block_levels(splits[5], (NSUB, LEV, NX, NY), ((0, 4), (2, 4), (3, 2)), -0.2, 0.2)), 0.3, 3.0)
    obs_var = jnp.clip(jnp.exp(math.log(2.0) - 1.3862944 * jax.random.uniform(splits[6], (NSUB, N_GX, N_GY, NOBS), jnp.float32) ** block_levels(splits[6], (NSUB, N_GX, N_GY, NOBS), ((0, 4), (1, 4), (2, 2)), -0.2, 0.2)), 0.5, 2.0)
    wind_east = jnp.clip(jax.random.uniform(splits[7], (NSUB, LEV, NX, NY), jnp.float32, -0.3, 0.3) * block_levels(splits[7], (NSUB, LEV, NX, NY), ((0, 4), (2, 4), (3, 2)), -0.4, 0.0), -0.3, 0.3)
    wind_north = jnp.clip(jax.random.uniform(splits[8], (NSUB, LEV, NX, NY), jnp.float32, -0.3, 0.3) * block_levels(splits[8], (NSUB, LEV, NX, NY), ((0, 4), (2, 4), (3, 2)), -0.4, 0.0), -0.3, 0.3)
    obs_cells = set_ends(jax.random.randint(splits[9], (NSUB, N_GX, N_GY, NOBS), 0, LEV * CX * CY), jax.random.fold_in(splits[9], 1), 0, (LEV * CX * CY) - 1).astype(jnp.int32)
    step_count = draw_step_count(jax.random.fold_in(splits[11], 71), 0)
    return {"lagrange": lagrange, "obs_lagrange": obs_lagrange, "increment": increment, "forcing": forcing, "departures": departures, "model_var": model_var, "obs_var": obs_var, "wind_east": wind_east, "wind_north": wind_north, "obs_cells": obs_cells, "step_count": step_count}


DIFFUSION = 0.18
VERTICAL = 0.1
CENTRE = 1.0 - 4.0 * DIFFUSION - 2.0 * VERTICAL


def coefficients(east_wind, north_wind):
    return (DIFFUSION - 0.5 * east_wind, DIFFUSION + 0.5 * east_wind,
            DIFFUSION - 0.5 * north_wind, DIFFUSION + 0.5 * north_wind)


def vertical_sum(field):
    padded = jnp.pad(field, ((1, 1), (0, 0), (0, 0)))
    return padded[2:] + padded[:-2]


def forward_step(field, coefs):
    east, west, north, south = coefs
    padded = jnp.pad(field, ((0, 0), (1, 1), (1, 1)))
    return (CENTRE * field + east * padded[:, 2:, 1:-1] + west * padded[:, :-2, 1:-1]
            + north * padded[:, 1:-1, 2:] + south * padded[:, 1:-1, :-2] + VERTICAL * vertical_sum(field))


def moved(term):
    return jnp.pad(term, ((0, 0), (1, 1), (1, 1)))


def adjoint_step(field, coefs):
    east, west, north, south = coefs
    return (CENTRE * field + moved(east * field)[:, :-2, 1:-1] + moved(west * field)[:, 2:, 1:-1]
            + moved(north * field)[:, 1:-1, :-2] + moved(south * field)[:, 1:-1, 2:] + VERTICAL * vertical_sum(field))


def sweep_one(packed, adjoint):
    field, east_wind, north_wind, count = packed
    coefs = coefficients(east_wind, north_wind)
    for step_index in range(MAXSTEP):
        stepped = adjoint_step(field, coefs) if adjoint else forward_step(field, coefs)
        field = jnp.where(step_index < count, stepped, field)
    return field


def sweep_all(fields, wind_east, wind_north, step_count, adjoint):
    return lax.map(lambda packed: sweep_one(packed, adjoint), (fields, wind_east, wind_north, step_count))


def to_tiles(field):
    shaped = field.reshape(NSUB, LEV, N_GX, CX, N_GY, CY).transpose(0, 2, 4, 1, 3, 5)
    return shaped.reshape(NSUB, N_GX, N_GY, LEV * CX * CY)


def from_tiles(tiles):
    shaped = tiles.reshape(NSUB, N_GX, N_GY, LEV, CX, CY).transpose(0, 3, 1, 4, 2, 5)
    return shaped.reshape(NSUB, LEV, N_GX * CX, N_GY * CY)


def observe(field, obs_cells):
    return jnp.take_along_axis(to_tiles(field), obs_cells, axis=3)


def spread(values, obs_cells):
    cells = LEV * CX * CY
    tile_ids = jnp.arange(NSUB * N_GX * N_GY, dtype=jnp.int32).reshape(NSUB, N_GX, N_GY, 1)
    flat = (tile_ids * cells + obs_cells).reshape(-1).astype(jnp.int32)
    summed = jnp.zeros((NSUB * N_GX * N_GY * cells,), jnp.float32).at[flat].add(values.reshape(-1))
    return from_tiles(summed.reshape(NSUB, N_GX, N_GY, cells))


def apply_operator(lagr, obs_lagr, incr, model_var, obs_var, wind_east, wind_north, obs_cells, step_count):
    forward = sweep_all(incr, wind_east, wind_north, step_count, False)
    previous = jnp.concatenate((jnp.zeros_like(forward[:1]), forward[:-1]), 0)
    following = jnp.concatenate((lagr[1:], jnp.zeros_like(lagr[:1])), 0)
    backward = sweep_all(following, wind_east, wind_north, step_count, True)
    model_part = model_var * lagr + (incr - previous)
    obs_part = obs_var * obs_lagr + observe(incr, obs_cells)
    incr_part = (lagr - backward) + spread(obs_lagr, obs_cells)
    return model_part, obs_part, incr_part


def reference(lagrange, obs_lagrange, increment, forcing, departures, model_var, obs_var,
              wind_east, wind_north, obs_cells, step_count):
    fixed = (model_var, obs_var, wind_east, wind_north, obs_cells, step_count)
    first = apply_operator(lagrange, obs_lagrange, increment, *fixed)
    resid = (forcing - first[0], departures - first[1], -first[2])
    image = apply_operator(resid[0], resid[1], resid[2], *fixed)
    cross = jnp.sum(resid[0] * image[0]) + jnp.sum(resid[1] * image[1]) + jnp.sum(resid[2] * image[2])
    square = jnp.sum(image[0] * image[0]) + jnp.sum(image[1] * image[1]) + jnp.sum(image[2] * image[2])
    alpha = cross / (square + 1e-6)
    return (lagrange + alpha * resid[0], obs_lagrange + alpha * resid[1], increment + alpha * resid[2],
            resid[0] - alpha * image[0], resid[1] - alpha * image[1], resid[2] - alpha * image[2])
```

```python
import functools

import jax
import jax.numpy as jnp
from jax import lax
from jax.experimental import pallas as pl
from jax.experimental.pallas import tpu as pltpu
from jax.sharding import PartitionSpec as P

MAXSTEP = 4
DIFFUSION = 0.18
VERTICAL = 0.1
CENTRE = 1.0 - 4.0 * DIFFUSION - 2.0 * VERTICAL
FORWARD, ADJOINT = 0, 1
LOW, HIGH, SIDE = 0, 1, 2
PAD = 8
MESH = pl.DeviceIdType.MESH
F32, BF16 = jnp.float32, jnp.bfloat16


def pieces(value):
    high = value.astype(BF16)
    rest = value - high.astype(F32)
    mid = rest.astype(BF16)
    low = (rest - mid.astype(F32)).astype(BF16)
    return high, mid, low


def kernel(
    sizes,
    lagr, obs_lagr, incr, forcing, depart, model_var, obs_var, wind_e, wind_n, cells, counts,
    res_m, res_o, res_v, img_m, img_o, img_v, alpha_out,
    field, half_e, half_n, onehot, spread_buf, next_lagr, next_model, next_image, arrived,
    last_image, row_out, row_in, col_out, col_in, part_out, part_in,
    send_sem, recv_sem, wide_send, wide_recv, part_send, part_recv,
):
    n_tm, n_gx, n_gy = sizes
    subs, levels, rows, lanes = incr.shape
    flat = levels * rows
    end = subs - 1
    inner = pl.ds(PAD, rows)
    before = pl.ds(PAD - 1, rows)
    after = pl.ds(PAD + 1, rows)
    tm, gx, gy = lax.axis_index("tm"), lax.axis_index("gx"), lax.axis_index("gy")
    lane = lax.broadcasted_iota(jnp.int32, (rows, lanes), 1)
    out_edge = jnp.where(gy == 0, lanes - 1, 0)
    sign = jnp.where(gy == 0, -1.0, 1.0)
    at_edge = lane == out_edge
    at_first, at_last = lane == 0, lane == lanes - 1

    row_in[...] = jnp.zeros_like(row_in)
    next_lagr[...] = jnp.zeros_like(next_lagr)
    next_model[...] = jnp.zeros_like(next_model)
    next_image[...] = jnp.zeros_like(next_image)
    arrived[...] = jnp.zeros_like(arrived)
    last_image[...] = jnp.zeros_like(last_image)

    barrier = pltpu.get_barrier_semaphore()
    peers = 0
    for axis, me, count in (("tm", tm, n_tm), ("gx", gx, n_gx), ("gy", gy, n_gy)):
        for k in range(1, count):
            pl.semaphore_signal(
                barrier, inc=1, device_id={axis: lax.rem(me + k, count)}, device_id_type=MESH
            )
            peers += 1
    pl.semaphore_wait(barrier, peers)

    def wide(index, src, dst, step):
        return pltpu.make_async_remote_copy(
            src_ref=src, dst_ref=dst, send_sem=wide_send.at[index], recv_sem=wide_recv.at[index],
            device_id={"tm": lax.rem(tm + step + n_tm, n_tm)}, device_id_type=MESH,
        )

    sent_lagr = wide(0, lagr.at[0], next_lagr, -1)
    sent_model = wide(1, img_m.at[0], next_model, -1)
    sent_forward = wide(2, field.at[FORWARD, 0, end, pl.ds(1, levels), inner], arrived, 1)
    sent_image = wide(3, img_m.at[0], next_image, -1)
    sent_last = wide(4, field.at[FORWARD, 0, end, pl.ds(1, levels), inner], last_image, 1)
    not_first, not_last = tm > 0, tm < n_tm - 1

    @pl.when(not_first)
    def _():
        sent_lagr.start()

    for s in range(subs):
        img_m[s] = forcing[s] - model_var[s] * lagr[s] - incr[s]

    @pl.when(not_first)
    def _():
        sent_model.start()

    half_e[...] = jnp.zeros_like(half_e)
    for s in range(subs):
        half_n[s] = 0.5 * wind_n[s]
        half_e[s, :, inner] = 0.5 * wind_e[s]
        half_e[s, :, PAD - 1 : PAD] = jnp.full((levels, 1, lanes), DIFFUSION - 1.0, F32)
        half_e[s, :, PAD + rows : PAD + rows + 1] = jnp.full((levels, 1, lanes), 1.0 - DIFFUSION, F32)
    for kind in (FORWARD, ADJOINT):
        for slot in range(2):
            for s in range(subs):
                for edge in (0, levels + 1):
                    field[kind, slot, s, edge] = jnp.zeros(field.shape[4:], F32)

    def sends(kind, turn):
        pairs = []
        for side, axis, to, allowed in (
            (LOW, "gx", lax.rem(gx + n_gx - 1, n_gx), gx > 0),
            (HIGH, "gx", lax.rem(gx + 1, n_gx), gx < n_gx - 1),
            (SIDE, "gy", lax.rem(gy + 1, n_gy), None),
        ):
            if side == SIDE:
                src, dst, back = col_out.at[kind, turn], col_in.at[kind, turn], None
            else:
                src, dst = row_out.at[kind, turn, side], row_in.at[kind, turn, 1 - side]
                back = gx < n_gx - 1 if side == LOW else gx > 0
            arrival = SIDE if side == SIDE else 1 - side
            copy = pltpu.make_async_remote_copy(
                src_ref=src, dst_ref=dst,
                send_sem=send_sem.at[kind, turn, side], recv_sem=recv_sem.at[kind, turn, arrival],
                device_id={axis: to}, device_id_type=MESH,
            )
            pairs.append((copy, allowed, back))
        return pairs

    def guarded(condition, action):
        if condition is None:
            action()
        else:
            pl.when(condition)(action)

    def start_halo(kind, turn):
        for copy, allowed, _ in sends(kind, turn):
            guarded(allowed, copy.start)

    def wait_halo(kind, turn):
        for copy, _, back in sends(kind, turn):
            guarded(back, copy.wait_recv)

    def put(kind, turn, slot, s, level, new, packed):
        field[kind, slot, s, level + 1, inner] = new
        first, last = new[0:1], new[rows - 1 : rows]
        edge = new
        if kind == ADJOINT:
            first = (DIFFUSION + half_e[s, level, PAD : PAD + 1]) * first
            last = (DIFFUSION - half_e[s, level, PAD + rows - 1 : PAD + rows]) * last
            edge = (DIFFUSION + sign * half_n[s, level]) * new
        row_out[kind, turn, LOW, s, level : level + 1] = first
        row_out[kind, turn, HIGH, s, level : level + 1] = last
        at = s * levels + level
        moved = pltpu.roll(edge, lax.rem(at - out_edge + lanes, lanes), 1)
        return jnp.where(lane == at, moved, packed)

    def begin(kind, turn, source):
        packed = jnp.zeros((rows, lanes), F32)
        for s in range(subs):
            for level in range(levels):
                packed = put(kind, turn, 0, s, level, source(s, level), packed)
        col_out[kind, turn] = packed
        start_halo(kind, turn)

    def step(kind, operator, j):
        turn = operator * MAXSTEP + j
        slot = lax.rem(j, 2)
        wait_halo(kind, turn)
        following = turn + 1
        packed = jnp.zeros((rows, lanes), F32)
        for s in range(subs):
            running = jnp.broadcast_to(counts[s], (rows, lanes)) > j
            for level in range(levels):
                field[kind, slot, s, level + 1, PAD - 1 : PAD] = (
                    row_in[kind, turn, LOW, s, level : level + 1]
                )
                field[kind, slot, s, level + 1, PAD + rows : PAD + rows + 1] = (
                    row_in[kind, turn, HIGH, s, level : level + 1]
                )
            for level in range(levels):
                at = s * levels + level
                here = field[kind, slot, s, level + 1, inner]
                east = field[kind, slot, s, level + 1, after]
                west = field[kind, slot, s, level + 1, before]
                column = pltpu.roll(col_in[kind, turn], lax.rem(out_edge - at + lanes, lanes), 1)
                column = jnp.where(at_edge, column, 0.0)
                level_sum = field[kind, slot, s, level + 2, inner] + field[kind, slot, s, level, inner]
                wind = half_n[s, level]
                if kind == FORWARD:
                    north = jnp.where(at_last, column, pltpu.roll(here, lanes - 1, 1))
                    south = jnp.where(at_first, column, pltpu.roll(here, 1, 1))
                    stepped = (
                        CENTRE * here
                        + DIFFUSION * ((east + west) + (north + south))
                        + half_e[s, level, inner] * (west - east)
                        + wind * (south - north)
                        + VERTICAL * level_sum
                    )
                else:
                    north = pltpu.roll((DIFFUSION + wind) * here, lanes - 1, 1)
                    south = pltpu.roll((DIFFUSION - wind) * here, 1, 1)
                    stepped = (
                        CENTRE * here
                        + (DIFFUSION - half_e[s, level, before]) * west
                        + (DIFFUSION + half_e[s, level, after]) * east
                        + jnp.where(at_first, column, south)
                        + jnp.where(at_last, column, north)
                        + VERTICAL * level_sum
                    )
                new = jnp.where(running, stepped, here)
                packed = put(kind, following, 1 - slot, s, level, new, packed)

        @pl.when(j < MAXSTEP - 1)
        def _():
            col_out[kind, following] = packed
            start_halo(kind, following)

    def sweeps(operator):
        def body(j, carry):
            step(FORWARD, operator, j)
            step(ADJOINT, operator, j)
            return carry

        lax.fori_loop(0, MAXSTEP, body, 0)

    def where_lane(s):
        return lax.broadcasted_iota(jnp.int32, (lanes, cells.shape[3]), 0) == lax.rem(cells[s, 0], lanes)

    def observe(s, value):
        turned = value.reshape(flat, lanes).T
        parts = jnp.concatenate(pieces(turned), 0)
        picked = jnp.dot(parts, onehot[s], preferred_element_type=F32)
        whole = (picked[:lanes] + picked[lanes : 2 * lanes]) + picked[2 * lanes :]
        return jnp.sum(jnp.where(where_lane(s), whole, 0.0), 0, keepdims=True)

    def spread(s, value):
        mask = where_lane(s)
        parts = jnp.concatenate(
            [jnp.where(mask, part.astype(F32), 0.0).astype(BF16) for part in pieces(value)], 0
        )
        summed = lax.dot_general(
            onehot[s], parts, (((1,), (1,)), ((), ())), preferred_element_type=F32
        )
        whole = (summed[:, :lanes] + summed[:, lanes : 2 * lanes]) + summed[:, 2 * lanes :]
        return whole.reshape(levels, rows, lanes)

    begin(FORWARD, 0, lambda s, level: incr[s, level])
    for s in range(subs):
        chosen = lax.div(cells[s, 0], lanes)
        place = lax.broadcasted_iota(jnp.int32, (flat, cells.shape[3]), 0)
        onehot[s] = jnp.where(place == chosen, 1.0, 0.0).astype(BF16)
    for s in range(subs):
        spread_buf[s] = spread(s, obs_lagr[s, 0])
        res_o[s, 0] = depart[s, 0] - (obs_var[s, 0] * obs_lagr[s, 0] + observe(s, incr[s]))

    @pl.when(not_last)
    def _():
        sent_lagr.wait_recv()

    begin(ADJOINT, 0, lambda s, level: lagr[s + 1, level] if s < end else next_lagr[level])
    sweeps(0)

    @pl.when(not_last)
    def _():
        sent_forward.start()
        sent_model.wait_recv()

    @pl.when(not_first)
    def _():
        sent_model.wait_send()

    live = jnp.where(not_last, 1.0, 0.0)
    for s in range(subs):
        res_v[s] = field[ADJOINT, 0, s, pl.ds(1, levels), inner] - lagr[s] - spread_buf[s]
    res_m[0] = img_m[0]
    for s in range(1, subs):
        res_m[s] = img_m[s] + field[FORWARD, 0, s - 1, pl.ds(1, levels), inner]
    next_model[...] = live * (next_model[...] + field[FORWARD, 0, end, pl.ds(1, levels), inner])

    @pl.when(not_last)
    def _():
        sent_forward.wait_send()

    begin(FORWARD, MAXSTEP, lambda s, level: res_v[s, level])
    begin(ADJOINT, MAXSTEP, lambda s, level: res_m[s + 1, level] if s < end else next_model[level])
    for s in range(subs):
        spread_buf[s] = spread(s, res_o[s, 0])
        img_o[s, 0] = obs_var[s, 0] * res_o[s, 0] + observe(s, res_v[s])

    @pl.when(not_first)
    def _():
        sent_forward.wait_recv()

    res_m[0] = res_m[0] + arrived[...]
    for s in range(subs):
        img_m[s] = model_var[s] * res_m[s] + res_v[s]

    @pl.when(not_first)
    def _():
        sent_image.start()

    sweeps(1)

    @pl.when(not_last)
    def _():
        sent_last.start()
        sent_image.wait_recv()

    cross = jnp.zeros((rows, lanes), F32)
    square = jnp.zeros((rows, lanes), F32)
    for s in range(subs):
        for level in range(levels):
            image = res_m[s, level] - field[ADJOINT, 0, s, level + 1, inner] + spread_buf[s, level]
            img_v[s, level] = image
            cross = cross + res_v[s, level] * image
            square = square + image * image
    for s in range(1, subs):
        for level in range(levels):
            image = img_m[s, level] - field[FORWARD, 0, s - 1, level + 1, inner]
            img_m[s, level] = image
            cross = cross + res_m[s, level] * image
            square = square + image * image
    alone = jnp.where(not_first, 0.0, 1.0)
    for level in range(levels):
        image = live * (next_image[level] - field[FORWARD, 0, end, level + 1, inner])
        cross = cross + next_model[level] * image
        square = square + image * image
        image = alone * img_m[0, level]
        cross = cross + res_m[0, level] * image
        square = square + image * image
    obs_cross = jnp.zeros((1, cells.shape[3]), F32)
    obs_square = jnp.zeros((1, cells.shape[3]), F32)
    for s in range(subs):
        obs_cross = obs_cross + res_o[s, 0] * img_o[s, 0]
        obs_square = obs_square + img_o[s, 0] * img_o[s, 0]

    def folded(grid, line):
        tile = jnp.sum(grid.reshape(rows // 8, 8, lanes), 0)
        for at in range(0, line.shape[1], lanes):
            piece = line[:, at : at + lanes]
            head = lax.broadcasted_iota(jnp.int32, (8, lanes), 0) == 0
            tile = tile + jnp.where(head, jnp.broadcast_to(piece, (8, lanes)), 0.0)
        return tile

    both = jnp.concatenate([folded(cross, obs_cross), folded(square, obs_square)], 0)
    base = 0
    for phase, (axis, me, count) in enumerate((("gx", gx, n_gx), ("gy", gy, n_gy), ("tm", tm, n_tm))):
        part_out[phase] = both
        copies = []
        for k in range(1, count):
            copy = pltpu.make_async_remote_copy(
                src_ref=part_out.at[phase], dst_ref=part_in.at[base],
                send_sem=part_send.at[base], recv_sem=part_recv.at[base],
                device_id={axis: lax.rem(me + k, count)}, device_id_type=MESH,
            )
            copy.start()
            copies.append((copy, base))
            base += 1
        for copy, slot in copies:
            copy.wait_recv()
            both = both + part_in[slot]
        for copy, _ in copies:
            copy.wait_send()
    total_cross = jnp.sum(jnp.sum(both[:8], 0, keepdims=True), 1, keepdims=True)
    total_square = jnp.sum(jnp.sum(both[8:], 0, keepdims=True), 1, keepdims=True)
    alpha_out[...] = jnp.broadcast_to(total_cross / (total_square + 1e-06), alpha_out.shape)

    @pl.when(not_first)
    def _():
        sent_last.wait_recv()
        sent_lagr.wait_send()
        sent_image.wait_send()

    img_m[0] = img_m[0] - last_image[...]

    @pl.when(not_last)
    def _():
        sent_last.wait_send()

    def drain(turn, carry):
        for kind in (FORWARD, ADJOINT):
            for copy, allowed, _ in sends(kind, turn):
                guarded(allowed, copy.wait_send)
        return carry

    lax.fori_loop(0, 2 * MAXSTEP, drain, 0)


def shards(sizes, *operands):
    lagrange, obs_lagrange, increment = operands[:3]
    subs, levels, rows, lanes = increment.shape
    nobs = obs_lagrange.shape[3]
    n_tm, n_gx, n_gy = sizes
    grid = jax.ShapeDtypeStruct(increment.shape, F32)
    line = jax.ShapeDtypeStruct(obs_lagrange.shape, F32)
    state = pltpu.VMEM((levels, rows, lanes), F32)
    turns = 2 * MAXSTEP
    partners = n_tm + n_gx + n_gy - 3
    vmem = pl.BlockSpec(memory_space=pltpu.VMEM)
    res_m, res_o, res_v, img_m, img_o, img_v, alpha = pl.pallas_call(
        functools.partial(kernel, sizes),
        out_shape=(grid, line, grid, grid, line, grid, jax.ShapeDtypeStruct((8, 128), F32)),
        in_specs=[vmem] * 10 + [pl.BlockSpec(memory_space=pltpu.SMEM)],
        out_specs=[vmem] * 7,
        scratch_shapes=[
            pltpu.VMEM((2, 2, subs, levels + 2, rows + 2 * PAD, lanes), F32),
            pltpu.VMEM((subs, levels, rows + 2 * PAD, lanes), F32),
            pltpu.VMEM((subs, levels, rows, lanes), F32),
            pltpu.VMEM((subs, levels * rows, nobs), BF16),
            pltpu.VMEM((subs, levels, rows, lanes), F32),
            state, state, state, state, state,
            pltpu.VMEM((2, turns + 1, 2, subs, levels, lanes), F32),
            pltpu.VMEM((2, turns, 2, subs, levels, lanes), F32),
            pltpu.VMEM((2, turns, rows, lanes), F32),
            pltpu.VMEM((2, turns, rows, lanes), F32),
            pltpu.VMEM((3, 16, lanes), F32),
            pltpu.VMEM((partners, 16, lanes), F32),
            pltpu.SemaphoreType.DMA((2, turns, 3)),
            pltpu.SemaphoreType.DMA((2, turns, 3)),
            pltpu.SemaphoreType.DMA((5,)),
            pltpu.SemaphoreType.DMA((5,)),
            pltpu.SemaphoreType.DMA((partners,)),
            pltpu.SemaphoreType.DMA((partners,)),
        ],
        compiler_params=pltpu.CompilerParams(
            collective_id=0, has_side_effects=True, vmem_limit_bytes=48 * 1024 * 1024
        ),
    )(*operands)
    alpha = alpha[0, 0]
    return (
        lagrange + alpha * res_m,
        obs_lagrange + alpha * res_o,
        increment + alpha * res_v,
        res_m - alpha * img_m,
        res_o - alpha * img_o,
        res_v - alpha * img_v,
    )


def solution(mesh):
    sizes = (mesh.shape["tm"], mesh.shape["gx"], mesh.shape["gy"])
    state, line = P("tm", None, "gx", "gy"), P("tm", "gx", "gy", None)
    return jax.shard_map(
        functools.partial(shards, sizes),
        mesh=mesh,
        in_specs=(state, line, state, state, line, state, line, state, state, line, P("tm")),
        out_specs=(state, line, state, state, line, state),
        check_vma=False,
    )
```

```python
import functools

import jax
import jax.numpy as jnp
from jax import lax
from jax.experimental import pallas as pl
from jax.experimental.pallas import tpu as pltpu
from jax.sharding import PartitionSpec as P

MAXSTEP = 4
DIFFUSION = 0.18
VERTICAL = 0.1
CENTRE = 1.0 - 4.0 * DIFFUSION - 2.0 * VERTICAL
FORWARD, ADJOINT = 0, 1
LOW, HIGH, SIDE = 0, 1, 2
PAD = 8
MESH = pl.DeviceIdType.MESH
F32, BF16 = jnp.float32, jnp.bfloat16


def pieces(value):
    high = value.astype(BF16)
    rest = value - high.astype(F32)
    mid = rest.astype(BF16)
    low = (rest - mid.astype(F32)).astype(BF16)
    return high, mid, low


def kernel(
    sizes,
    lagr_in, obs_lagr_in, incr_in, forcing_in, depart_in, model_var_in, obs_var_in, wind_e_in, wind_n_in,
    cells_in, counts,
    res_m, res_o, res_v, img_m, img_o, img_v, alpha_grid, alpha_line,
    lagr, obs_lagr, incr, forcing, depart, model_var, obs_var, wind_e, wind_n, cells, load_sem,
    field, half_e, half_n, onehot, spread_buf, next_lagr, next_model, next_image, arrived,
    last_image, leaving, row_out, row_in, col_out, col_in, part_out, part_in,
    send_sem, recv_sem, wide_send, wide_recv, part_send, part_recv,
):
    n_tm, n_gx, n_gy = sizes
    subs, levels, rows, lanes = incr.shape
    flat = levels * rows
    end = subs - 1
    inner = pl.ds(PAD, rows)
    before = pl.ds(PAD - 1, rows)
    after = pl.ds(PAD + 1, rows)
    tm, gx, gy = lax.axis_index("tm"), lax.axis_index("gx"), lax.axis_index("gy")
    lane = lax.broadcasted_iota(jnp.int32, (rows, lanes), 1)
    out_edge = jnp.where(gy == 0, lanes - 1, 0)
    sign = jnp.where(gy == 0, -1.0, 1.0)
    at_edge = lane == out_edge
    at_first, at_last = lane == 0, lane == lanes - 1

    loads = [
        pltpu.make_async_copy(src, dst, load_sem.at[at])
        for at, (src, dst) in enumerate((
            (incr_in, incr), (lagr_in, lagr), (wind_e_in, wind_e), (wind_n_in, wind_n),
            (cells_in, cells), (model_var_in, model_var), (forcing_in, forcing),
            (obs_lagr_in, obs_lagr), (obs_var_in, obs_var), (depart_in, depart),
        ))
    ]
    for load in loads:
        load.start()

    row_in[...] = jnp.zeros_like(row_in)
    next_lagr[...] = jnp.zeros_like(next_lagr)
    next_model[...] = jnp.zeros_like(next_model)
    next_image[...] = jnp.zeros_like(next_image)
    arrived[...] = jnp.zeros_like(arrived)
    last_image[...] = jnp.zeros_like(last_image)

    plane = [
        {"gx": lax.rem(gx + a, n_gx), "gy": lax.rem(gy + b, n_gy)}
        for a in range(n_gx) for b in range(n_gy) if a + b > 0
    ]
    column_peers = [{"tm": lax.rem(tm + k, n_tm)} for k in range(1, n_tm)]
    barrier = pltpu.get_barrier_semaphore()
    for peer in plane + column_peers:
        pl.semaphore_signal(barrier, inc=1, device_id=peer, device_id_type=MESH)

    def wide(index, src, dst, step):
        return pltpu.make_async_remote_copy(
            src_ref=src, dst_ref=dst, send_sem=wide_send.at[index], recv_sem=wide_recv.at[index],
            device_id={"tm": lax.rem(tm + step + n_tm, n_tm)}, device_id_type=MESH,
        )

    sent_lagr = wide(0, lagr.at[0], next_lagr, -1)
    sent_model = wide(1, img_m.at[0], next_model, -1)
    sent_forward = wide(2, leaving, arrived, 1)
    sent_image = wide(3, img_m.at[0], next_image, -1)
    sent_last = wide(4, field.at[FORWARD, 0, end, pl.ds(1, levels), inner], last_image, 1)
    not_first, not_last = tm > 0, tm < n_tm - 1

    def sends(kind, turn):
        pairs = []
        for side, axis, to, allowed in (
            (LOW, "gx", lax.rem(gx + n_gx - 1, n_gx), gx > 0),
            (HIGH, "gx", lax.rem(gx + 1, n_gx), gx < n_gx - 1),
            (SIDE, "gy", lax.rem(gy + 1, n_gy), None),
        ):
            if side == SIDE:
                src, dst, back = col_out.at[kind, turn], col_in.at[kind, turn], None
            else:
                src, dst = row_out.at[kind, turn, side], row_in.at[kind, turn, 1 - side]
                back = gx < n_gx - 1 if side == LOW else gx > 0
            arrival = SIDE if side == SIDE else 1 - side
            copy = pltpu.make_async_remote_copy(
                src_ref=src, dst_ref=dst,
                send_sem=send_sem.at[kind, turn, side], recv_sem=recv_sem.at[kind, turn, arrival],
                device_id={axis: to}, device_id_type=MESH,
            )
            pairs.append((copy, allowed, back))
        return pairs

    def guarded(condition, action):
        if condition is None:
            action()
        else:
            pl.when(condition)(action)

    def start_halo(kind, turn):
        for copy, allowed, _ in sends(kind, turn):
            guarded(allowed, copy.start)

    def wait_halo(kind, turn):
        for copy, _, back in sends(kind, turn):
            guarded(back, copy.wait_recv)

    def put(kind, turn, slot, s, level, new, packed):
        field[kind, slot, s, level + 1, inner] = new
        first, last = new[0:1], new[rows - 1 : rows]
        edge = new
        if kind == ADJOINT:
            first = (DIFFUSION + half_e[s, level, PAD : PAD + 1]) * first
            last = (DIFFUSION - half_e[s, level, PAD + rows - 1 : PAD + rows]) * last
            edge = (DIFFUSION + sign * half_n[s, level]) * new
        row_out[kind, turn, LOW, s, level : level + 1] = first
        row_out[kind, turn, HIGH, s, level : level + 1] = last
        at = s * levels + level
        moved = pltpu.roll(edge, lax.rem(at - out_edge + lanes, lanes), 1)
        return jnp.where(lane == at, moved, packed)

    def begin(kind, turn, source):
        packed = jnp.zeros((rows, lanes), F32)
        for s in range(subs):
            for level in range(levels):
                packed = put(kind, turn, 0, s, level, source(s, level), packed)
        col_out[kind, turn] = packed

    def step(kind, operator, j):
        turn = operator * MAXSTEP + j
        slot = lax.rem(j, 2)
        wait_halo(kind, turn)
        following = turn + 1
        packed = jnp.zeros((rows, lanes), F32)
        for s in range(subs):
            running = jnp.broadcast_to(counts[s], (rows, lanes)) > j
            for level in range(levels):
                field[kind, slot, s, level + 1, PAD - 1 : PAD] = (
                    row_in[kind, turn, LOW, s, level : level + 1]
                )
                field[kind, slot, s, level + 1, PAD + rows : PAD + rows + 1] = (
                    row_in[kind, turn, HIGH, s, level : level + 1]
                )
            for level in range(levels):
                at = s * levels + level
                here = field[kind, slot, s, level + 1, inner]
                east = field[kind, slot, s, level + 1, after]
                west = field[kind, slot, s, level + 1, before]
                column = pltpu.roll(col_in[kind, turn], lax.rem(out_edge - at + lanes, lanes), 1)
                column = jnp.where(at_edge, column, 0.0)
                level_sum = field[kind, slot, s, level + 2, inner] + field[kind, slot, s, level, inner]
                wind = half_n[s, level]
                if kind == FORWARD:
                    north = jnp.where(at_last, column, pltpu.roll(here, lanes - 1, 1))
                    south = jnp.where(at_first, column, pltpu.roll(here, 1, 1))
                    stepped = (
                        CENTRE * here
                        + DIFFUSION * ((east + west) + (north + south))
                        + half_e[s, level, inner] * (west - east)
                        + wind * (south - north)
                        + VERTICAL * level_sum
                    )
                else:
                    north = pltpu.roll((DIFFUSION + wind) * here, lanes - 1, 1)
                    south = pltpu.roll((DIFFUSION - wind) * here, 1, 1)
                    stepped = (
                        CENTRE * here
                        + (DIFFUSION - half_e[s, level, before]) * west
                        + (DIFFUSION + half_e[s, level, after]) * east
                        + jnp.where(at_first, column, south)
                        + jnp.where(at_last, column, north)
                        + VERTICAL * level_sum
                    )
                new = jnp.where(running, stepped, here)
                packed = put(kind, following, 1 - slot, s, level, new, packed)

        @pl.when(j < MAXSTEP - 1)
        def _():
            col_out[kind, following] = packed
            start_halo(kind, following)

    def where_lane(s):
        return lax.broadcasted_iota(jnp.int32, (lanes, cells.shape[3]), 0) == lax.rem(cells[s, 0], lanes)

    def observe(s, value):
        turned = value.reshape(flat, lanes).T
        parts = jnp.concatenate(pieces(turned), 0)
        picked = jnp.dot(parts, onehot[s], preferred_element_type=F32)
        whole = (picked[:lanes] + picked[lanes : 2 * lanes]) + picked[2 * lanes :]
        return jnp.sum(jnp.where(where_lane(s), whole, 0.0), 0, keepdims=True)

    def spread(s, value):
        mask = where_lane(s)
        parts = jnp.concatenate(
            [jnp.where(mask, part.astype(F32), 0.0).astype(BF16) for part in pieces(value)], 0
        )
        summed = lax.dot_general(
            onehot[s], parts, (((1,), (1,)), ((), ())), preferred_element_type=F32
        )
        whole = (summed[:, :lanes] + summed[:, lanes : 2 * lanes]) + summed[:, 2 * lanes :]
        return whole.reshape(levels, rows, lanes)

    def sweeps(operator, first_work, second_work):
        def body(pair, carry):
            for half, work in enumerate((first_work, second_work)):
                j = pair * 2 + half
                step(FORWARD, operator, j)
                work(pair)
                step(ADJOINT, operator, j)
            return carry

        lax.fori_loop(0, MAXSTEP // 2, body, 0)

    for kind in (FORWARD, ADJOINT):
        for slot in range(2):
            for s in range(subs):
                for edge in (0, levels + 1):
                    field[kind, slot, s, edge] = jnp.zeros(field.shape[4:], F32)
    loads[0].wait()
    begin(FORWARD, 0, lambda s, level: incr[s, level])
    loads[1].wait()
    pl.semaphore_wait(barrier, len(plane) + len(column_peers))

    @pl.when(not_first)
    def _():
        sent_lagr.start()

    start_halo(FORWARD, 0)
    loads[5].wait()
    loads[6].wait()
    for s in range(subs):
        img_m[s] = forcing[s] - model_var[s] * lagr[s] - incr[s]

    @pl.when(not_first)
    def _():
        sent_model.start()

    loads[2].wait()
    loads[3].wait()
    half_e[...] = jnp.zeros_like(half_e)
    for s in range(subs):
        half_n[s] = 0.5 * wind_n[s]
        half_e[s, :, inner] = 0.5 * wind_e[s]
        half_e[s, :, PAD - 1 : PAD] = jnp.full((levels, 1, lanes), DIFFUSION - 1.0, F32)
        half_e[s, :, PAD + rows : PAD + rows + 1] = jnp.full((levels, 1, lanes), 1.0 - DIFFUSION, F32)
    loads[4].wait()
    for s in range(subs):
        chosen = lax.div(cells[s, 0], lanes)
        place = lax.broadcasted_iota(jnp.int32, (flat, cells.shape[3]), 0)
        onehot[s] = jnp.where(place == chosen, 1.0, 0.0).astype(BF16)
    for load in loads[7:]:
        load.wait()

    @pl.when(not_last)
    def _():
        sent_lagr.wait_recv()

    begin(ADJOINT, 0, lambda s, level: lagr[s + 1, level] if s < end else next_lagr[level])
    start_halo(ADJOINT, 0)

    def first_spread(s):
        spread_buf[s] = spread(s, obs_lagr[s, 0])

    def first_observe(s):
        res_o[s, 0] = depart[s, 0] - (obs_var[s, 0] * obs_lagr[s, 0] + observe(s, incr[s]))

    sweeps(0, first_spread, first_observe)
    leaving[...] = field[FORWARD, 0, end, pl.ds(1, levels), inner]

    @pl.when(not_last)
    def _():
        sent_forward.start()
        sent_model.wait_recv()

    @pl.when(not_first)
    def _():
        sent_model.wait_send()

    live = jnp.where(not_last, 1.0, 0.0)
    for s in range(subs):
        res_v[s] = field[ADJOINT, 0, s, pl.ds(1, levels), inner] - lagr[s] - spread_buf[s]
    res_m[0] = img_m[0]
    for s in range(1, subs):
        res_m[s] = img_m[s] + field[FORWARD, 0, s - 1, pl.ds(1, levels), inner]
    next_model[...] = live * (next_model[...] + field[FORWARD, 0, end, pl.ds(1, levels), inner])

    begin(FORWARD, MAXSTEP, lambda s, level: res_v[s, level])
    start_halo(FORWARD, MAXSTEP)
    begin(ADJOINT, MAXSTEP, lambda s, level: res_m[s + 1, level] if s < end else next_model[level])
    start_halo(ADJOINT, MAXSTEP)

    def second_spread(s):
        spread_buf[s] = spread(s, res_o[s, 0])

    def second_observe(s):
        img_o[s, 0] = obs_var[s, 0] * res_o[s, 0] + observe(s, res_v[s])

    @pl.when(not_first)
    def _():
        sent_forward.wait_recv()

    res_m[0] = res_m[0] + arrived[...]
    for s in range(subs):
        img_m[s] = model_var[s] * res_m[s] + res_v[s]

    @pl.when(not_first)
    def _():
        sent_image.start()

    sweeps(1, second_spread, second_observe)

    @pl.when(not_last)
    def _():
        sent_last.start()
        sent_image.wait_recv()

    cross = jnp.zeros((rows, lanes), F32)
    square = jnp.zeros((rows, lanes), F32)
    for s in range(subs):
        for level in range(levels):
            image = res_m[s, level] - field[ADJOINT, 0, s, level + 1, inner] + spread_buf[s, level]
            img_v[s, level] = image
            cross = cross + res_v[s, level] * image
            square = square + image * image
    for s in range(1, subs):
        for level in range(levels):
            image = img_m[s, level] - field[FORWARD, 0, s - 1, level + 1, inner]
            img_m[s, level] = image
            cross = cross + res_m[s, level] * image
            square = square + image * image
    alone = jnp.where(not_first, 0.0, 1.0)
    for level in range(levels):
        image = live * (next_image[level] - field[FORWARD, 0, end, level + 1, inner])
        cross = cross + next_model[level] * image
        square = square + image * image
        image = alone * img_m[0, level]
        cross = cross + res_m[0, level] * image
        square = square + image * image
    obs_cross = jnp.zeros((1, cells.shape[3]), F32)
    obs_square = jnp.zeros((1, cells.shape[3]), F32)
    for s in range(subs):
        obs_cross = obs_cross + res_o[s, 0] * img_o[s, 0]
        obs_square = obs_square + img_o[s, 0] * img_o[s, 0]

    def folded(grid, line):
        tile = jnp.sum(grid.reshape(rows // 8, 8, lanes), 0)
        for at in range(0, line.shape[1], lanes):
            piece = line[:, at : at + lanes]
            head = lax.broadcasted_iota(jnp.int32, (8, lanes), 0) == 0
            tile = tile + jnp.where(head, jnp.broadcast_to(piece, (8, lanes)), 0.0)
        return tile

    both = jnp.concatenate([folded(cross, obs_cross), folded(square, obs_square)], 0)
    base = 0
    for phase, targets in enumerate((plane, column_peers)):
        part_out[phase] = both
        copies = []
        for target in targets:
            copy = pltpu.make_async_remote_copy(
                src_ref=part_out.at[phase], dst_ref=part_in.at[base],
                send_sem=part_send.at[base], recv_sem=part_recv.at[base],
                device_id=target, device_id_type=MESH,
            )
            copy.start()
            copies.append((copy, base))
            base += 1
        for copy, slot in copies:
            copy.wait_recv()
            both = both + part_in[slot]
        for copy, _ in copies:
            copy.wait_send()
    total_cross = jnp.sum(jnp.sum(both[:8], 0, keepdims=True), 1, keepdims=True)
    total_square = jnp.sum(jnp.sum(both[8:], 0, keepdims=True), 1, keepdims=True)
    alpha = total_cross / (total_square + 1e-06)
    alpha_grid[0, 0] = jnp.broadcast_to(alpha, alpha_grid.shape[2:])
    alpha_line[0, 0] = jnp.broadcast_to(alpha, alpha_line.shape[2:])

    @pl.when(not_first)
    def _():
        sent_last.wait_recv()
        sent_lagr.wait_send()
        sent_image.wait_send()

    img_m[0] = img_m[0] - last_image[...]

    @pl.when(not_last)
    def _():
        sent_forward.wait_send()
        sent_last.wait_send()

    def drain(turn, carry):
        for kind in (FORWARD, ADJOINT):
            for copy, allowed, _ in sends(kind, turn):
                guarded(allowed, copy.wait_send)
        return carry

    lax.fori_loop(0, 2 * MAXSTEP, drain, 0)


def shards(sizes, *operands):
    lagrange, obs_lagrange, increment = operands[:3]
    subs, levels, rows, lanes = increment.shape
    nobs = obs_lagrange.shape[3]
    n_tm, n_gx, n_gy = sizes
    grid = jax.ShapeDtypeStruct(increment.shape, F32)
    line = jax.ShapeDtypeStruct(obs_lagrange.shape, F32)
    state = pltpu.VMEM((levels, rows, lanes), F32)
    turns = 2 * MAXSTEP
    partners = n_gx * n_gy - 1 + n_tm - 1
    vmem = pl.BlockSpec(memory_space=pltpu.VMEM)
    hbm = pl.BlockSpec(memory_space=pltpu.HBM)
    res_m, res_o, res_v, img_m, img_o, img_v, alpha, alpha_line = pl.pallas_call(
        functools.partial(kernel, sizes),
        out_shape=(grid, line, grid, grid, line, grid, jax.ShapeDtypeStruct((1, 1, 1, lanes), F32),
                   jax.ShapeDtypeStruct((1, 1, 1, nobs), F32)),
        in_specs=[hbm] * 10 + [pl.BlockSpec(memory_space=pltpu.SMEM)],
        out_specs=[vmem] * 8,
        scratch_shapes=[
            *(pltpu.VMEM(operand.shape, operand.dtype) for operand in operands[:10]),
            pltpu.SemaphoreType.DMA((10,)),
            pltpu.VMEM((2, 2, subs, levels + 2, rows + 2 * PAD, lanes), F32),
            pltpu.VMEM((subs, levels, rows + 2 * PAD, lanes), F32),
            pltpu.VMEM((subs, levels, rows, lanes), F32),
            pltpu.VMEM((subs, levels * rows, nobs), BF16),
            pltpu.VMEM((subs, levels, rows, lanes), F32),
            state, state, state, state, state, state,
            pltpu.VMEM((2, turns + 1, 2, subs, levels, lanes), F32),
            pltpu.VMEM((2, turns, 2, subs, levels, lanes), F32),
            pltpu.VMEM((2, turns, rows, lanes), F32),
            pltpu.VMEM((2, turns, rows, lanes), F32),
            pltpu.VMEM((2, 16, lanes), F32),
            pltpu.VMEM((partners, 16, lanes), F32),
            pltpu.SemaphoreType.DMA((2, turns, 3)),
            pltpu.SemaphoreType.DMA((2, turns, 3)),
            pltpu.SemaphoreType.DMA((5,)),
            pltpu.SemaphoreType.DMA((5,)),
            pltpu.SemaphoreType.DMA((partners,)),
            pltpu.SemaphoreType.DMA((partners,)),
        ],
        compiler_params=pltpu.CompilerParams(
            collective_id=0, has_side_effects=True, vmem_limit_bytes=60 * 1024 * 1024
        ),
    )(*operands)
    return (
        lagrange + alpha * res_m,
        obs_lagrange + alpha_line * res_o,
        increment + alpha * res_v,
        res_m - alpha * img_m,
        res_o - alpha_line * img_o,
        res_v - alpha * img_v,
    )


def solution(mesh):
    sizes = (mesh.shape["tm"], mesh.shape["gx"], mesh.shape["gy"])
    state, line = P("tm", None, "gx", "gy"), P("tm", "gx", "gy", None)
    return jax.shard_map(
        functools.partial(shards, sizes),
        mesh=mesh,
        in_specs=(state, line, state, state, line, state, line, state, state, line, P("tm")),
        out_specs=(state, line, state, state, line, state),
        check_vma=False,
    )
```

```python
import functools

import jax
import jax.numpy as jnp
from jax import lax
from jax.experimental import pallas as pl
from jax.experimental.pallas import tpu as pltpu
from jax.sharding import PartitionSpec as P

MAXSTEP = 4
DIFFUSION = 0.18
VERTICAL = 0.1
CENTRE = 1.0 - 4.0 * DIFFUSION - 2.0 * VERTICAL
FORWARD, ADJOINT = 0, 1
LOW, HIGH, SIDE = 0, 1, 2
PAD = 8
MESH = pl.DeviceIdType.MESH
F32, BF16 = jnp.float32, jnp.bfloat16


def pieces(value):
    high = value.astype(BF16)
    rest = value - high.astype(F32)
    mid = rest.astype(BF16)
    low = (rest - mid.astype(F32)).astype(BF16)
    return high, mid, low


def kernel(
    sizes,
    lagr_in, obs_lagr_in, incr_in, forcing_in, depart_in, model_var_in, obs_var_in, wind_e_in, wind_n_in,
    cells_in, counts,
    res_m, res_o, res_v, img_m, img_o, img_v, alpha_grid, alpha_line,
    lagr, obs_lagr, incr, forcing, depart, model_var, obs_var, wind_e, wind_n, cells, load_sem,
    field_00, field_01, field_10, field_11, half_e, half_n, onehot, spread_buf, next_lagr, next_model, next_image, arrived,
    last_image, leaving, row_out, row_in, col_out, col_in, part_out, part_in,
    send_sem, recv_sem, wide_send, wide_recv, part_send, part_recv,
):
    n_tm, n_gx, n_gy = sizes
    subs, levels, rows, lanes = incr.shape
    flat = levels * rows
    end = subs - 1
    field = ((field_00, field_01), (field_10, field_11))
    inner = pl.ds(PAD, rows)
    before = pl.ds(PAD - 1, rows)
    after = pl.ds(PAD + 1, rows)
    tm, gx, gy = lax.axis_index("tm"), lax.axis_index("gx"), lax.axis_index("gy")
    lane = lax.broadcasted_iota(jnp.int32, (rows, lanes), 1)
    out_edge = jnp.where(gy == 0, lanes - 1, 0)
    sign = jnp.where(gy == 0, -1.0, 1.0)
    at_edge = lane == out_edge
    at_first, at_last = lane == 0, lane == lanes - 1

    loads = [
        pltpu.make_async_copy(src, dst, load_sem.at[at])
        for at, (src, dst) in enumerate((
            (incr_in, incr), (lagr_in, lagr), (wind_e_in, wind_e), (wind_n_in, wind_n),
            (cells_in, cells), (model_var_in, model_var), (forcing_in, forcing),
            (obs_lagr_in, obs_lagr), (obs_var_in, obs_var), (depart_in, depart),
        ))
    ]
    for load in loads:
        load.start()

    row_in[...] = jnp.zeros_like(row_in)
    next_lagr[...] = jnp.zeros_like(next_lagr)
    next_model[...] = jnp.zeros_like(next_model)
    next_image[...] = jnp.zeros_like(next_image)
    arrived[...] = jnp.zeros_like(arrived)
    last_image[...] = jnp.zeros_like(last_image)

    plane = [
        {"gx": lax.rem(gx + a, n_gx), "gy": lax.rem(gy + b, n_gy)}
        for a in range(n_gx) for b in range(n_gy) if a + b > 0
    ]
    column_peers = [{"tm": lax.rem(tm + k, n_tm)} for k in range(1, n_tm)]
    barrier = pltpu.get_barrier_semaphore()
    for peer in plane + column_peers:
        pl.semaphore_signal(barrier, inc=1, device_id=peer, device_id_type=MESH)

    def wide(index, src, dst, step):
        return pltpu.make_async_remote_copy(
            src_ref=src, dst_ref=dst, send_sem=wide_send.at[index], recv_sem=wide_recv.at[index],
            device_id={"tm": lax.rem(tm + step + n_tm, n_tm)}, device_id_type=MESH,
        )

    sent_lagr = wide(0, lagr.at[0], next_lagr, -1)
    sent_model = wide(1, img_m.at[0], next_model, -1)
    sent_forward = wide(2, leaving, arrived, 1)
    sent_image = wide(3, img_m.at[0], next_image, -1)
    sent_last = wide(4, field_00.at[end, pl.ds(1, levels), inner], last_image, 1)
    not_first, not_last = tm > 0, tm < n_tm - 1

    def sends(kind, turn):
        pairs = []
        for side, axis, to, allowed in (
            (LOW, "gx", lax.rem(gx + n_gx - 1, n_gx), gx > 0),
            (HIGH, "gx", lax.rem(gx + 1, n_gx), gx < n_gx - 1),
            (SIDE, "gy", lax.rem(gy + 1, n_gy), None),
        ):
            if side == SIDE:
                src, dst, back = col_out.at[kind, turn], col_in.at[kind, turn], None
            else:
                src, dst = row_out.at[kind, turn, side], row_in.at[kind, turn, 1 - side]
                back = gx < n_gx - 1 if side == LOW else gx > 0
            arrival = SIDE if side == SIDE else 1 - side
            copy = pltpu.make_async_remote_copy(
                src_ref=src, dst_ref=dst,
                send_sem=send_sem.at[kind, turn, side], recv_sem=recv_sem.at[kind, turn, arrival],
                device_id={axis: to}, device_id_type=MESH,
            )
            pairs.append((copy, allowed, back))
        return pairs

    def guarded(condition, action):
        if condition is None:
            action()
        else:
            pl.when(condition)(action)

    def start_halo(kind, turn):
        for copy, allowed, _ in sends(kind, turn):
            guarded(allowed, copy.start)

    def wait_halo(kind, turn):
        for copy, _, back in sends(kind, turn):
            guarded(back, copy.wait_recv)

    def put(kind, turn, slot, s, level, new, packed):
        field[kind][slot][s, level + 1, inner] = new
        first, last = new[0:1], new[rows - 1 : rows]
        edge = new
        if kind == ADJOINT:
            first = (DIFFUSION + half_e[s, level, PAD : PAD + 1]) * first
            last = (DIFFUSION - half_e[s, level, PAD + rows - 1 : PAD + rows]) * last
            edge = (DIFFUSION + sign * half_n[s, level]) * new
        row_out[kind, turn, LOW, s, level : level + 1] = first
        row_out[kind, turn, HIGH, s, level : level + 1] = last
        at = s * levels + level
        moved = pltpu.roll(edge, lax.rem(at - out_edge + lanes, lanes), 1)
        return jnp.where(lane == at, moved, packed)

    def begin(kind, turn, source):
        packed = jnp.zeros((rows, lanes), F32)
        for s in range(subs):
            for level in range(levels):
                packed = put(kind, turn, 0, s, level, source(s, level), packed)
        col_out[kind, turn] = packed

    def step(kind, operator, j, slot):
        turn = operator * MAXSTEP + j
        wait_halo(kind, turn)
        following = turn + 1
        packed = jnp.zeros((rows, lanes), F32)
        for s in range(subs):
            running = jnp.broadcast_to(counts[s], (rows, lanes)) > j
            for level in range(levels):
                field[kind][slot][s, level + 1, PAD - 1 : PAD] = (
                    row_in[kind, turn, LOW, s, level : level + 1]
                )
                field[kind][slot][s, level + 1, PAD + rows : PAD + rows + 1] = (
                    row_in[kind, turn, HIGH, s, level : level + 1]
                )
            for level in range(levels):
                at = s * levels + level
                here = field[kind][slot][s, level + 1, inner]
                east = field[kind][slot][s, level + 1, after]
                west = field[kind][slot][s, level + 1, before]
                column = pltpu.roll(col_in[kind, turn], lax.rem(out_edge - at + lanes, lanes), 1)
                column = jnp.where(at_edge, column, 0.0)
                level_sum = field[kind][slot][s, level + 2, inner] + field[kind][slot][s, level, inner]
                wind = half_n[s, level]
                if kind == FORWARD:
                    north = jnp.where(at_last, column, pltpu.roll(here, lanes - 1, 1))
                    south = jnp.where(at_first, column, pltpu.roll(here, 1, 1))
                    stepped = (
                        CENTRE * here
                        + DIFFUSION * ((east + west) + (north + south))
                        + half_e[s, level, inner] * (west - east)
                        + wind * (south - north)
                        + VERTICAL * level_sum
                    )
                else:
                    north = pltpu.roll((DIFFUSION + wind) * here, lanes - 1, 1)
                    south = pltpu.roll((DIFFUSION - wind) * here, 1, 1)
                    stepped = (
                        CENTRE * here
                        + (DIFFUSION - half_e[s, level, before]) * west
                        + (DIFFUSION + half_e[s, level, after]) * east
                        + jnp.where(at_first, column, south)
                        + jnp.where(at_last, column, north)
                        + VERTICAL * level_sum
                    )
                new = jnp.where(running, stepped, here)
                packed = put(kind, following, 1 - slot, s, level, new, packed)

        @pl.when(j < MAXSTEP - 1)
        def _():
            col_out[kind, following] = packed
            start_halo(kind, following)

    def where_lane(s):
        return lax.broadcasted_iota(jnp.int32, (lanes, cells.shape[3]), 0) == lax.rem(cells[s, 0], lanes)

    def observe(s, value):
        turned = value.reshape(flat, lanes).T
        parts = jnp.concatenate(pieces(turned), 0)
        picked = jnp.dot(parts, onehot[s], preferred_element_type=F32)
        whole = (picked[:lanes] + picked[lanes : 2 * lanes]) + picked[2 * lanes :]
        return jnp.sum(jnp.where(where_lane(s), whole, 0.0), 0, keepdims=True)

    def spread(s, value):
        mask = where_lane(s)
        parts = jnp.concatenate(
            [jnp.where(mask, part.astype(F32), 0.0).astype(BF16) for part in pieces(value)], 0
        )
        summed = lax.dot_general(
            onehot[s], parts, (((1,), (1,)), ((), ())), preferred_element_type=F32
        )
        whole = (summed[:, :lanes] + summed[:, lanes : 2 * lanes]) + summed[:, 2 * lanes :]
        return whole.reshape(levels, rows, lanes)

    def sweeps(operator, first_work, second_work):
        def body(pair, carry):
            for half, work in enumerate((first_work, second_work)):
                j = pair * 2 + half
                step(FORWARD, operator, j, half)
                work(pair)
                step(ADJOINT, operator, j, half)
            return carry

        lax.fori_loop(0, MAXSTEP // 2, body, 0)

    for kind in (FORWARD, ADJOINT):
        for slot in range(2):
            for s in range(subs):
                for edge in (0, levels + 1):
                    field[kind][slot][s, edge] = jnp.zeros(field_00.shape[2:], F32)
    loads[0].wait()
    begin(FORWARD, 0, lambda s, level: incr[s, level])
    loads[1].wait()
    pl.semaphore_wait(barrier, len(plane) + len(column_peers))

    @pl.when(not_first)
    def _():
        sent_lagr.start()

    start_halo(FORWARD, 0)
    loads[5].wait()
    loads[6].wait()
    for s in range(subs):
        img_m[s] = forcing[s] - model_var[s] * lagr[s] - incr[s]

    @pl.when(not_first)
    def _():
        sent_model.start()

    loads[2].wait()
    loads[3].wait()
    half_e[...] = jnp.zeros_like(half_e)
    for s in range(subs):
        half_n[s] = 0.5 * wind_n[s]
        half_e[s, :, inner] = 0.5 * wind_e[s]
        half_e[s, :, PAD - 1 : PAD] = jnp.full((levels, 1, lanes), DIFFUSION - 1.0, F32)
        half_e[s, :, PAD + rows : PAD + rows + 1] = jnp.full((levels, 1, lanes), 1.0 - DIFFUSION, F32)
    loads[4].wait()
    for s in range(subs):
        chosen = lax.div(cells[s, 0], lanes)
        place = lax.broadcasted_iota(jnp.int32, (flat, cells.shape[3]), 0)
        onehot[s] = jnp.where(place == chosen, 1.0, 0.0).astype(BF16)
    for load in loads[7:]:
        load.wait()

    @pl.when(not_last)
    def _():
        sent_lagr.wait_recv()

    begin(ADJOINT, 0, lambda s, level: lagr[s + 1, level] if s < end else next_lagr[level])
    start_halo(ADJOINT, 0)

    def first_spread(s):
        spread_buf[s] = spread(s, obs_lagr[s, 0])

    def first_observe(s):
        res_o[s, 0] = depart[s, 0] - (obs_var[s, 0] * obs_lagr[s, 0] + observe(s, incr[s]))

    sweeps(0, first_spread, first_observe)
    leaving[...] = field[FORWARD][0][end, pl.ds(1, levels), inner]

    @pl.when(not_last)
    def _():
        sent_forward.start()
        sent_model.wait_recv()

    @pl.when(not_first)
    def _():
        sent_model.wait_send()

    live = jnp.where(not_last, 1.0, 0.0)
    for s in range(subs):
        res_v[s] = field[ADJOINT][0][s, pl.ds(1, levels), inner] - lagr[s] - spread_buf[s]
    res_m[0] = img_m[0]
    for s in range(1, subs):
        res_m[s] = img_m[s] + field[FORWARD][0][s - 1, pl.ds(1, levels), inner]
    next_model[...] = live * (next_model[...] + field[FORWARD][0][end, pl.ds(1, levels), inner])

    begin(FORWARD, MAXSTEP, lambda s, level: res_v[s, level])
    start_halo(FORWARD, MAXSTEP)
    begin(ADJOINT, MAXSTEP, lambda s, level: res_m[s + 1, level] if s < end else next_model[level])
    start_halo(ADJOINT, MAXSTEP)

    def second_spread(s):
        spread_buf[s] = spread(s, res_o[s, 0])

    def second_observe(s):
        img_o[s, 0] = obs_var[s, 0] * res_o[s, 0] + observe(s, res_v[s])

    @pl.when(not_first)
    def _():
        sent_forward.wait_recv()

    res_m[0] = res_m[0] + arrived[...]
    for s in range(subs):
        img_m[s] = model_var[s] * res_m[s] + res_v[s]

    @pl.when(not_first)
    def _():
        sent_image.start()

    sweeps(1, second_spread, second_observe)

    @pl.when(not_last)
    def _():
        sent_last.start()
        sent_image.wait_recv()

    cross = jnp.zeros((rows, lanes), F32)
    square = jnp.zeros((rows, lanes), F32)
    for s in range(subs):
        for level in range(levels):
            image = res_m[s, level] - field[ADJOINT][0][s, level + 1, inner] + spread_buf[s, level]
            img_v[s, level] = image
            cross = cross + res_v[s, level] * image
            square = square + image * image
    for s in range(1, subs):
        for level in range(levels):
            image = img_m[s, level] - field[FORWARD][0][s - 1, level + 1, inner]
            img_m[s, level] = image
            cross = cross + res_m[s, level] * image
            square = square + image * image
    alone = jnp.where(not_first, 0.0, 1.0)
    for level in range(levels):
        image = live * (next_image[level] - field[FORWARD][0][end, level + 1, inner])
        cross = cross + next_model[level] * image
        square = square + image * image
        image = alone * img_m[0, level]
        cross = cross + res_m[0, level] * image
        square = square + image * image
    obs_cross = jnp.zeros((1, cells.shape[3]), F32)
    obs_square = jnp.zeros((1, cells.shape[3]), F32)
    for s in range(subs):
        obs_cross = obs_cross + res_o[s, 0] * img_o[s, 0]
        obs_square = obs_square + img_o[s, 0] * img_o[s, 0]

    def folded(grid, line):
        tile = jnp.sum(grid.reshape(rows // 8, 8, lanes), 0)
        for at in range(0, line.shape[1], lanes):
            piece = line[:, at : at + lanes]
            head = lax.broadcasted_iota(jnp.int32, (8, lanes), 0) == 0
            tile = tile + jnp.where(head, jnp.broadcast_to(piece, (8, lanes)), 0.0)
        return tile

    both = jnp.concatenate([folded(cross, obs_cross), folded(square, obs_square)], 0)
    base = 0
    for phase, targets in enumerate((plane, column_peers)):
        part_out[phase] = both
        copies = []
        for target in targets:
            copy = pltpu.make_async_remote_copy(
                src_ref=part_out.at[phase], dst_ref=part_in.at[base],
                send_sem=part_send.at[base], recv_sem=part_recv.at[base],
                device_id=target, device_id_type=MESH,
            )
            copy.start()
            copies.append((copy, base))
            base += 1
        for copy, slot in copies:
            copy.wait_recv()
            both = both + part_in[slot]
        for copy, _ in copies:
            copy.wait_send()
    total_cross = jnp.sum(jnp.sum(both[:8], 0, keepdims=True), 1, keepdims=True)
    total_square = jnp.sum(jnp.sum(both[8:], 0, keepdims=True), 1, keepdims=True)
    alpha = total_cross / (total_square + 1e-06)
    alpha_grid[0, 0] = jnp.broadcast_to(alpha, alpha_grid.shape[2:])
    alpha_line[0, 0] = jnp.broadcast_to(alpha, alpha_line.shape[2:])

    @pl.when(not_first)
    def _():
        sent_last.wait_recv()
        sent_lagr.wait_send()
        sent_image.wait_send()

    img_m[0] = img_m[0] - last_image[...]

    @pl.when(not_last)
    def _():
        sent_forward.wait_send()
        sent_last.wait_send()

    def drain(turn, carry):
        for kind in (FORWARD, ADJOINT):
            for copy, allowed, _ in sends(kind, turn):
                guarded(allowed, copy.wait_send)
        return carry

    lax.fori_loop(0, 2 * MAXSTEP, drain, 0)


def update(*refs):
    sources, targets, held, made = refs[:11], refs[11:17], refs[17:28], refs[28:34]
    load_sem, small_sem, store_sem = refs[34:]
    subs = held[0].shape[0]
    small = [pltpu.make_async_copy(sources[6 + at], held[6 + at], small_sem.at[at]) for at in range(5)]
    loads = [
        [pltpu.make_async_copy(sources[at].at[s], held[at].at[s], load_sem.at[at, s]) for at in range(6)]
        for s in range(subs)
    ]
    stores = [
        [pltpu.make_async_copy(made[at].at[s], targets[at].at[s], store_sem.at[at, s]) for at in range(6)]
        for s in range(subs)
    ]
    small[3].start()
    for group in loads:
        for load in group:
            load.start()
    for at in (0, 1, 2, 4):
        small[at].start()
    lagr, incr, res_m, res_v, img_m, img_v, obs_lagr, res_o, img_o, alpha_grid, alpha_line = held
    small[3].wait()
    alpha = alpha_grid[0]
    for s in range(subs):
        for load in loads[s]:
            load.wait()
        made[0][s] = lagr[s] + alpha * res_m[s]
        stores[s][0].start()
        made[2][s] = incr[s] + alpha * res_v[s]
        stores[s][2].start()
        made[3][s] = res_m[s] - alpha * img_m[s]
        stores[s][3].start()
        made[5][s] = res_v[s] - alpha * img_v[s]
        stores[s][5].start()
    for at in (0, 1, 2, 4):
        small[at].wait()
    for s in range(subs):
        made[1][s] = obs_lagr[s] + alpha_line[0] * res_o[s]
        stores[s][1].start()
        made[4][s] = res_o[s] - alpha_line[0] * img_o[s]
        stores[s][4].start()
    for group in stores:
        for store in group:
            store.wait()


def shards(sizes, *operands):
    lagrange, obs_lagrange, increment = operands[:3]
    subs, levels, rows, lanes = increment.shape
    nobs = obs_lagrange.shape[3]
    n_tm, n_gx, n_gy = sizes
    grid = jax.ShapeDtypeStruct(increment.shape, F32)
    line = jax.ShapeDtypeStruct(obs_lagrange.shape, F32)
    state = pltpu.VMEM((levels, rows, lanes), F32)
    turns = 2 * MAXSTEP
    partners = n_gx * n_gy - 1 + n_tm - 1
    vmem = pl.BlockSpec(memory_space=pltpu.VMEM)
    hbm = pl.BlockSpec(memory_space=pltpu.HBM)
    res_m, res_o, res_v, img_m, img_o, img_v, alpha, alpha_line = pl.pallas_call(
        functools.partial(kernel, sizes),
        out_shape=(grid, line, grid, grid, line, grid, jax.ShapeDtypeStruct((1, 1, 1, lanes), F32),
                   jax.ShapeDtypeStruct((1, 1, 1, nobs), F32)),
        in_specs=[hbm] * 10 + [pl.BlockSpec(memory_space=pltpu.SMEM)],
        out_specs=[vmem] * 8,
        scratch_shapes=[
            *(pltpu.VMEM(operand.shape, operand.dtype) for operand in operands[:10]),
            pltpu.SemaphoreType.DMA((10,)),
            *[pltpu.VMEM((subs, levels + 2, rows + 2 * PAD, lanes), F32)] * 4,
            pltpu.VMEM((subs, levels, rows + 2 * PAD, lanes), F32),
            pltpu.VMEM((subs, levels, rows, lanes), F32),
            pltpu.VMEM((subs, levels * rows, nobs), BF16),
            pltpu.VMEM((subs, levels, rows, lanes), F32),
            state, state, state, state, state, state,
            pltpu.VMEM((2, turns + 1, 2, subs, levels, lanes), F32),
            pltpu.VMEM((2, turns, 2, subs, levels, lanes), F32),
            pltpu.VMEM((2, turns, rows, lanes), F32),
            pltpu.VMEM((2, turns, rows, lanes), F32),
            pltpu.VMEM((2, 16, lanes), F32),
            pltpu.VMEM((partners, 16, lanes), F32),
            pltpu.SemaphoreType.DMA((2, turns, 3)),
            pltpu.SemaphoreType.DMA((2, turns, 3)),
            pltpu.SemaphoreType.DMA((5,)),
            pltpu.SemaphoreType.DMA((5,)),
            pltpu.SemaphoreType.DMA((partners,)),
            pltpu.SemaphoreType.DMA((partners,)),
        ],
        compiler_params=pltpu.CompilerParams(
            collective_id=0, has_side_effects=True, vmem_limit_bytes=60 * 1024 * 1024
        ),
    )(*operands)
    sources = (lagrange, increment, res_m, res_v, img_m, img_v, obs_lagrange, res_o, img_o, alpha, alpha_line)
    return pl.pallas_call(
        update,
        out_shape=(grid, line, grid, grid, line, grid),
        in_specs=[hbm] * len(sources),
        out_specs=[hbm] * 6,
        scratch_shapes=[
            *(pltpu.VMEM(source.shape, source.dtype) for source in sources),
            *(pltpu.VMEM(shape.shape, F32) for shape in (grid, line, grid, grid, line, grid)),
            pltpu.SemaphoreType.DMA((6, subs)),
            pltpu.SemaphoreType.DMA((5,)),
            pltpu.SemaphoreType.DMA((6, subs)),
        ],
        compiler_params=pltpu.CompilerParams(vmem_limit_bytes=60 * 1024 * 1024),
    )(*sources)


def solution(mesh):
    sizes = (mesh.shape["tm"], mesh.shape["gx"], mesh.shape["gy"])
    state, line = P("tm", None, "gx", "gy"), P("tm", "gx", "gy", None)
    return jax.shard_map(
        functools.partial(shards, sizes),
        mesh=mesh,
        in_specs=(state, line, state, state, line, state, line, state, state, line, P("tm")),
        out_specs=(state, line, state, state, line, state),
        check_vma=False,
    )
```

```python
import functools

import jax
import jax.numpy as jnp
from jax import lax
from jax.experimental import pallas as pl
from jax.experimental.pallas import tpu as pltpu
from jax.sharding import PartitionSpec as P

MAXSTEP = 4
DIFFUSION = 0.18
VERTICAL = 0.1
CENTRE = 1.0 - 4.0 * DIFFUSION - 2.0 * VERTICAL
FORWARD, ADJOINT = 0, 1
LOW, HIGH, SIDE = 0, 1, 2
PAD = 8
MESH = pl.DeviceIdType.MESH
F32, BF16 = jnp.float32, jnp.bfloat16


def pieces(value):
    high = value.astype(BF16)
    rest = value - high.astype(F32)
    mid = rest.astype(BF16)
    low = (rest - mid.astype(F32)).astype(BF16)
    return high, mid, low


def kernel(
    sizes,
    lagr_in, obs_lagr_in, incr_in, forcing_in, depart_in, model_var_in, obs_var_in, wind_e_in, wind_n_in,
    cells_in, counts,
    res_m, res_o, res_v, img_m, img_o, img_v, alpha_grid, alpha_line,
    lagr, obs_lagr, incr, forcing, depart, model_var, obs_var, wind_e, wind_n, cells, load_sem,
    field_00, field_01, field_10, field_11, half_e, half_n, from_west, from_east, later, onehot, spread_buf, next_lagr, next_model, next_image, arrived,
    last_image, leaving, row_out, row_in, col_out, col_in, part_out, part_in,
    send_sem, recv_sem, wide_send, wide_recv, part_send, part_recv,
):
    n_tm, n_gx, n_gy = sizes
    subs, levels, rows, lanes = incr.shape
    flat = levels * rows
    end = subs - 1
    field = ((field_00, field_01), (field_10, field_11))
    inner = pl.ds(PAD, rows)
    before = pl.ds(PAD - 1, rows)
    after = pl.ds(PAD + 1, rows)
    tm, gx, gy = lax.axis_index("tm"), lax.axis_index("gx"), lax.axis_index("gy")
    lane = lax.broadcasted_iota(jnp.int32, (rows, lanes), 1)
    out_edge = jnp.where(gy == 0, lanes - 1, 0)
    sign = jnp.where(gy == 0, -1.0, 1.0)
    at_edge = lane == out_edge
    at_first, at_last = lane == 0, lane == lanes - 1

    loads = [
        pltpu.make_async_copy(src, dst, load_sem.at[at])
        for at, (src, dst) in enumerate((
            (incr_in, incr), (lagr_in, lagr), (wind_e_in, wind_e), (wind_n_in, wind_n),
            (cells_in, cells), (model_var_in, model_var), (forcing_in, forcing),
            (obs_lagr_in, obs_lagr), (obs_var_in, obs_var), (depart_in, depart),
        ))
    ]
    for load in loads:
        load.start()

    row_in[...] = jnp.zeros_like(row_in)
    next_lagr[...] = jnp.zeros_like(next_lagr)
    next_model[...] = jnp.zeros_like(next_model)
    next_image[...] = jnp.zeros_like(next_image)
    arrived[...] = jnp.zeros_like(arrived)
    last_image[...] = jnp.zeros_like(last_image)

    plane = [
        {"gx": lax.rem(gx + a, n_gx), "gy": lax.rem(gy + b, n_gy)}
        for a in range(n_gx) for b in range(n_gy) if a + b > 0
    ]
    column_peers = [{"tm": lax.rem(tm + k, n_tm)} for k in range(1, n_tm)]
    barrier = pltpu.get_barrier_semaphore()
    for peer in plane + column_peers:
        pl.semaphore_signal(barrier, inc=1, device_id=peer, device_id_type=MESH)

    def wide(index, src, dst, step):
        return pltpu.make_async_remote_copy(
            src_ref=src, dst_ref=dst, send_sem=wide_send.at[index], recv_sem=wide_recv.at[index],
            device_id={"tm": lax.rem(tm + step + n_tm, n_tm)}, device_id_type=MESH,
        )

    sent_lagr = wide(0, lagr.at[0], next_lagr, -1)
    sent_model = wide(1, img_m.at[0], next_model, -1)
    sent_forward = wide(2, leaving, arrived, 1)
    sent_image = wide(3, img_m.at[0], next_image, -1)
    sent_last = wide(4, field_00.at[end, pl.ds(1, levels), inner], last_image, 1)
    not_first, not_last = tm > 0, tm < n_tm - 1

    def sends(kind, turn):
        pairs = []
        for side, axis, to, allowed in (
            (LOW, "gx", lax.rem(gx + n_gx - 1, n_gx), gx > 0),
            (HIGH, "gx", lax.rem(gx + 1, n_gx), gx < n_gx - 1),
            (SIDE, "gy", lax.rem(gy + 1, n_gy), None),
        ):
            if side == SIDE:
                src, dst, back = col_out.at[kind, turn], col_in.at[kind, turn], None
            else:
                src, dst = row_out.at[kind, turn, side], row_in.at[kind, turn, 1 - side]
                back = gx < n_gx - 1 if side == LOW else gx > 0
            arrival = SIDE if side == SIDE else 1 - side
            copy = pltpu.make_async_remote_copy(
                src_ref=src, dst_ref=dst,
                send_sem=send_sem.at[kind, turn, side], recv_sem=recv_sem.at[kind, turn, arrival],
                device_id={axis: to}, device_id_type=MESH,
            )
            pairs.append((copy, allowed, back))
        return pairs

    def guarded(condition, action):
        if condition is None:
            action()
        else:
            pl.when(condition)(action)

    def start_halo(kind, turn):
        for copy, allowed, _ in sends(kind, turn):
            guarded(allowed, copy.start)

    def wait_halo(kind, turn):
        for copy, _, back in sends(kind, turn):
            guarded(back, copy.wait_recv)

    def put(kind, turn, slot, s, level, new, packed):
        field[kind][slot][s, level + 1, inner] = new
        first, last = new[0:1], new[rows - 1 : rows]
        edge = new
        if kind == ADJOINT:
            first = (DIFFUSION + half_e[s, level, PAD : PAD + 1]) * first
            last = (DIFFUSION - half_e[s, level, PAD + rows - 1 : PAD + rows]) * last
            edge = (DIFFUSION + sign * half_n[s, level]) * new
        row_out[kind, turn, LOW, s, pl.ds(level, 1)] = first
        row_out[kind, turn, HIGH, s, pl.ds(level, 1)] = last
        at = s * levels + level
        moved = pltpu.roll(edge, lax.rem(at - out_edge + lanes, lanes), 1)
        return jnp.where(lane == at, moved, packed)

    def over_levels(visit):
        group = 4
        turns_of = levels // group

        def body(at, packed):
            s, first = lax.div(at, turns_of), lax.rem(at, turns_of) * group
            for k in range(group):
                packed = visit(s, first + k, packed)
            return packed

        return lax.fori_loop(0, subs * turns_of, body, jnp.zeros((rows, lanes), F32))

    def begin(kind, turn, source):
        def visit(s, level, packed):
            return put(kind, turn, 0, s, level, source[s, level], packed)

        col_out[kind, turn] = over_levels(visit)

    def step(kind, operator, j, slot):
        turn = operator * MAXSTEP + j
        wait_halo(kind, turn)
        following = turn + 1
        source = field[kind][slot]

        def visit(s, level, packed):
            source[s, level + 1, PAD - 1 : PAD] = row_in[kind, turn, LOW, s, pl.ds(level, 1)]
            source[s, level + 1, PAD + rows : PAD + rows + 1] = row_in[kind, turn, HIGH, s, pl.ds(level, 1)]
            running = jnp.broadcast_to(counts[s], (rows, lanes)) > j
            at = s * levels + level
            here = source[s, level + 1, inner]
            east = source[s, level + 1, after]
            west = source[s, level + 1, before]
            column = pltpu.roll(col_in[kind, turn], lax.rem(out_edge - at + lanes, lanes), 1)
            column = jnp.where(at_edge, column, 0.0)
            level_sum = source[s, level + 2, inner] + source[s, level, inner]
            wind = half_n[s, level]
            if kind == FORWARD:
                north = jnp.where(at_last, column, pltpu.roll(here, lanes - 1, 1))
                south = jnp.where(at_first, column, pltpu.roll(here, 1, 1))
                stepped = (
                    CENTRE * here
                    + DIFFUSION * ((east + west) + (north + south))
                    + half_e[s, level, inner] * (west - east)
                    + wind * (south - north)
                    + VERTICAL * level_sum
                )
            else:
                north = pltpu.roll((DIFFUSION + wind) * here, lanes - 1, 1)
                south = pltpu.roll((DIFFUSION - wind) * here, 1, 1)
                stepped = (
                    CENTRE * here
                    + from_west[s, level] * west
                    + from_east[s, level] * east
                    + jnp.where(at_first, column, south)
                    + jnp.where(at_last, column, north)
                    + VERTICAL * level_sum
                )
            new = jnp.where(running, stepped, here)
            return put(kind, following, 1 - slot, s, level, new, packed)

        packed = over_levels(visit)

        @pl.when(j < MAXSTEP - 1)
        def _():
            col_out[kind, following] = packed
            start_halo(kind, following)

    def where_lane(s):
        return lax.broadcasted_iota(jnp.int32, (lanes, cells.shape[3]), 0) == lax.rem(cells[s, 0], lanes)

    def observe(s, value):
        turned = value.reshape(flat, lanes).T
        parts = jnp.concatenate(pieces(turned), 0)
        picked = jnp.dot(parts, onehot[s], preferred_element_type=F32)
        whole = (picked[:lanes] + picked[lanes : 2 * lanes]) + picked[2 * lanes :]
        return jnp.sum(jnp.where(where_lane(s), whole, 0.0), 0, keepdims=True)

    def spread(s, value):
        mask = where_lane(s)
        parts = jnp.concatenate(
            [jnp.where(mask, part.astype(F32), 0.0).astype(BF16) for part in pieces(value)], 0
        )
        summed = lax.dot_general(
            onehot[s], parts, (((1,), (1,)), ((), ())), preferred_element_type=F32
        )
        whole = (summed[:, :lanes] + summed[:, lanes : 2 * lanes]) + summed[:, 2 * lanes :]
        return whole.reshape(levels, rows, lanes)

    def sweeps(operator, first_work, second_work):
        def body(pair, carry):
            for half, work in enumerate((first_work, second_work)):
                j = pair * 2 + half
                step(FORWARD, operator, j, half)
                work(pair)
                step(ADJOINT, operator, j, half)
            return carry

        lax.fori_loop(0, MAXSTEP // 2, body, 0)

    for kind in (FORWARD, ADJOINT):
        for slot in range(2):
            for s in range(subs):
                for edge in (0, levels + 1):
                    field[kind][slot][s, edge] = jnp.zeros(field_00.shape[2:], F32)
    loads[0].wait()
    begin(FORWARD, 0, incr)
    loads[1].wait()
    pl.semaphore_wait(barrier, len(plane) + len(column_peers))

    @pl.when(not_first)
    def _():
        sent_lagr.start()

    start_halo(FORWARD, 0)
    loads[5].wait()
    loads[6].wait()
    for s in range(subs):
        img_m[s] = forcing[s] - model_var[s] * lagr[s] - incr[s]

    @pl.when(not_first)
    def _():
        sent_model.start()

    loads[2].wait()
    loads[3].wait()
    half_e[...] = jnp.zeros_like(half_e)
    for s in range(subs):
        half_n[s] = 0.5 * wind_n[s]
        half_e[s, :, inner] = 0.5 * wind_e[s]
        half_e[s, :, PAD - 1 : PAD] = jnp.full((levels, 1, lanes), DIFFUSION - 1.0, F32)
        half_e[s, :, PAD + rows : PAD + rows + 1] = jnp.full((levels, 1, lanes), 1.0 - DIFFUSION, F32)
    for s in range(subs):
        from_west[s] = DIFFUSION - half_e[s, :, before]
        from_east[s] = DIFFUSION + half_e[s, :, after]
    loads[4].wait()
    for s in range(subs):
        chosen = lax.div(cells[s, 0], lanes)
        place = lax.broadcasted_iota(jnp.int32, (flat, cells.shape[3]), 0)
        onehot[s] = jnp.where(place == chosen, 1.0, 0.0).astype(BF16)
    for load in loads[7:]:
        load.wait()

    @pl.when(not_last)
    def _():
        sent_lagr.wait_recv()

    for s in range(end):
        later[s] = lagr[s + 1]
    later[end] = next_lagr[...]
    begin(ADJOINT, 0, later)
    start_halo(ADJOINT, 0)

    def first_spread(s):
        spread_buf[s] = spread(s, obs_lagr[s, 0])

    def first_observe(s):
        res_o[s, 0] = depart[s, 0] - (obs_var[s, 0] * obs_lagr[s, 0] + observe(s, incr[s]))

    sweeps(0, first_spread, first_observe)
    leaving[...] = field[FORWARD][0][end, pl.ds(1, levels), inner]

    @pl.when(not_last)
    def _():
        sent_forward.start()
        sent_model.wait_recv()

    @pl.when(not_first)
    def _():
        sent_model.wait_send()

    live = jnp.where(not_last, 1.0, 0.0)
    for s in range(subs):
        res_v[s] = field[ADJOINT][0][s, pl.ds(1, levels), inner] - lagr[s] - spread_buf[s]
    res_m[0] = img_m[0]
    for s in range(1, subs):
        res_m[s] = img_m[s] + field[FORWARD][0][s - 1, pl.ds(1, levels), inner]
    next_model[...] = live * (next_model[...] + field[FORWARD][0][end, pl.ds(1, levels), inner])

    begin(FORWARD, MAXSTEP, res_v)
    start_halo(FORWARD, MAXSTEP)
    for s in range(end):
        later[s] = res_m[s + 1]
    later[end] = next_model[...]
    begin(ADJOINT, MAXSTEP, later)
    start_halo(ADJOINT, MAXSTEP)

    def second_spread(s):
        spread_buf[s] = spread(s, res_o[s, 0])

    def second_observe(s):
        img_o[s, 0] = obs_var[s, 0] * res_o[s, 0] + observe(s, res_v[s])

    @pl.when(not_first)
    def _():
        sent_forward.wait_recv()

    res_m[0] = res_m[0] + arrived[...]
    for s in range(subs):
        img_m[s] = model_var[s] * res_m[s] + res_v[s]

    @pl.when(not_first)
    def _():
        sent_image.start()

    sweeps(1, second_spread, second_observe)

    @pl.when(not_last)
    def _():
        sent_last.start()
        sent_image.wait_recv()

    cross = jnp.zeros((rows, lanes), F32)
    square = jnp.zeros((rows, lanes), F32)
    for s in range(subs):
        for level in range(levels):
            image = res_m[s, level] - field[ADJOINT][0][s, level + 1, inner] + spread_buf[s, level]
            img_v[s, level] = image
            cross = cross + res_v[s, level] * image
            square = square + image * image
    for s in range(1, subs):
        for level in range(levels):
            image = img_m[s, level] - field[FORWARD][0][s - 1, level + 1, inner]
            img_m[s, level] = image
            cross = cross + res_m[s, level] * image
            square = square + image * image
    alone = jnp.where(not_first, 0.0, 1.0)
    for level in range(levels):
        image = live * (next_image[level] - field[FORWARD][0][end, level + 1, inner])
        cross = cross + next_model[level] * image
        square = square + image * image
        image = alone * img_m[0, level]
        cross = cross + res_m[0, level] * image
        square = square + image * image
    obs_cross = jnp.zeros((1, cells.shape[3]), F32)
    obs_square = jnp.zeros((1, cells.shape[3]), F32)
    for s in range(subs):
        obs_cross = obs_cross + res_o[s, 0] * img_o[s, 0]
        obs_square = obs_square + img_o[s, 0] * img_o[s, 0]

    def folded(grid, line):
        tile = jnp.sum(grid.reshape(rows // 8, 8, lanes), 0)
        for at in range(0, line.shape[1], lanes):
            piece = line[:, at : at + lanes]
            head = lax.broadcasted_iota(jnp.int32, (8, lanes), 0) == 0
            tile = tile + jnp.where(head, jnp.broadcast_to(piece, (8, lanes)), 0.0)
        return tile

    both = jnp.concatenate([folded(cross, obs_cross), folded(square, obs_square)], 0)
    base = 0
    for phase, targets in enumerate((plane, column_peers)):
        part_out[phase] = both
        copies = []
        for target in targets:
            copy = pltpu.make_async_remote_copy(
                src_ref=part_out.at[phase], dst_ref=part_in.at[base],
                send_sem=part_send.at[base], recv_sem=part_recv.at[base],
                device_id=target, device_id_type=MESH,
            )
            copy.start()
            copies.append((copy, base))
            base += 1
        for copy, slot in copies:
            copy.wait_recv()
            both = both + part_in[slot]
        for copy, _ in copies:
            copy.wait_send()
    total_cross = jnp.sum(jnp.sum(both[:8], 0, keepdims=True), 1, keepdims=True)
    total_square = jnp.sum(jnp.sum(both[8:], 0, keepdims=True), 1, keepdims=True)
    alpha = total_cross / (total_square + 1e-06)
    alpha_grid[0, 0] = jnp.broadcast_to(alpha, alpha_grid.shape[2:])
    alpha_line[0, 0] = jnp.broadcast_to(alpha, alpha_line.shape[2:])

    @pl.when(not_first)
    def _():
        sent_last.wait_recv()
        sent_lagr.wait_send()
        sent_image.wait_send()

    img_m[0] = img_m[0] - last_image[...]

    @pl.when(not_last)
    def _():
        sent_forward.wait_send()
        sent_last.wait_send()

    def drain(turn, carry):
        for kind in (FORWARD, ADJOINT):
            for copy, allowed, _ in sends(kind, turn):
                guarded(allowed, copy.wait_send)
        return carry

    lax.fori_loop(0, 2 * MAXSTEP, drain, 0)


def update(*refs):
    sources, targets, held, made = refs[:11], refs[11:17], refs[17:28], refs[28:34]
    load_sem, small_sem, store_sem = refs[34:]
    subs = held[0].shape[0]
    small = [pltpu.make_async_copy(sources[6 + at], held[6 + at], small_sem.at[at]) for at in range(5)]
    loads = [
        [pltpu.make_async_copy(sources[at].at[s], held[at].at[s], load_sem.at[at, s]) for at in range(6)]
        for s in range(subs)
    ]
    stores = [
        [pltpu.make_async_copy(made[at].at[s], targets[at].at[s], store_sem.at[at, s]) for at in range(6)]
        for s in range(subs)
    ]
    small[3].start()
    for group in loads:
        for load in group:
            load.start()
    for at in (0, 1, 2, 4):
        small[at].start()
    lagr, incr, res_m, res_v, img_m, img_v, obs_lagr, res_o, img_o, alpha_grid, alpha_line = held
    small[3].wait()
    alpha = alpha_grid[0]
    for s in range(subs):
        for load in loads[s]:
            load.wait()
        made[0][s] = lagr[s] + alpha * res_m[s]
        stores[s][0].start()
        made[2][s] = incr[s] + alpha * res_v[s]
        stores[s][2].start()
        made[3][s] = res_m[s] - alpha * img_m[s]
        stores[s][3].start()
        made[5][s] = res_v[s] - alpha * img_v[s]
        stores[s][5].start()
    for at in (0, 1, 2, 4):
        small[at].wait()
    for s in range(subs):
        made[1][s] = obs_lagr[s] + alpha_line[0] * res_o[s]
        stores[s][1].start()
        made[4][s] = res_o[s] - alpha_line[0] * img_o[s]
        stores[s][4].start()
    for group in stores:
        for store in group:
            store.wait()


def shards(sizes, *operands):
    lagrange, obs_lagrange, increment = operands[:3]
    subs, levels, rows, lanes = increment.shape
    nobs = obs_lagrange.shape[3]
    n_tm, n_gx, n_gy = sizes
    grid = jax.ShapeDtypeStruct(increment.shape, F32)
    line = jax.ShapeDtypeStruct(obs_lagrange.shape, F32)
    state = pltpu.VMEM((levels, rows, lanes), F32)
    turns = 2 * MAXSTEP
    partners = n_gx * n_gy - 1 + n_tm - 1
    vmem = pl.BlockSpec(memory_space=pltpu.VMEM)
    hbm = pl.BlockSpec(memory_space=pltpu.HBM)
    res_m, res_o, res_v, img_m, img_o, img_v, alpha, alpha_line = pl.pallas_call(
        functools.partial(kernel, sizes),
        out_shape=(grid, line, grid, grid, line, grid, jax.ShapeDtypeStruct((1, 1, 1, lanes), F32),
                   jax.ShapeDtypeStruct((1, 1, 1, nobs), F32)),
        in_specs=[hbm] * 10 + [pl.BlockSpec(memory_space=pltpu.SMEM)],
        out_specs=[vmem] * 8,
        scratch_shapes=[
            *(pltpu.VMEM(operand.shape, operand.dtype) for operand in operands[:10]),
            pltpu.SemaphoreType.DMA((10,)),
            *[pltpu.VMEM((subs, levels + 2, rows + 2 * PAD, lanes), F32)] * 4,
            pltpu.VMEM((subs, levels, rows + 2 * PAD, lanes), F32),
            *[pltpu.VMEM((subs, levels, rows, lanes), F32)] * 4,
            pltpu.VMEM((subs, levels * rows, nobs), BF16),
            pltpu.VMEM((subs, levels, rows, lanes), F32),
            state, state, state, state, state, state,
            pltpu.VMEM((2, turns + 1, 2, subs, levels, lanes), F32),
            pltpu.VMEM((2, turns, 2, subs, levels, lanes), F32),
            pltpu.VMEM((2, turns, rows, lanes), F32),
            pltpu.VMEM((2, turns, rows, lanes), F32),
            pltpu.VMEM((2, 16, lanes), F32),
            pltpu.VMEM((partners, 16, lanes), F32),
            pltpu.SemaphoreType.DMA((2, turns, 3)),
            pltpu.SemaphoreType.DMA((2, turns, 3)),
            pltpu.SemaphoreType.DMA((5,)),
            pltpu.SemaphoreType.DMA((5,)),
            pltpu.SemaphoreType.DMA((partners,)),
            pltpu.SemaphoreType.DMA((partners,)),
        ],
        compiler_params=pltpu.CompilerParams(
            collective_id=0, has_side_effects=True, vmem_limit_bytes=60 * 1024 * 1024
        ),
    )(*operands)
    sources = (lagrange, increment, res_m, res_v, img_m, img_v, obs_lagrange, res_o, img_o, alpha, alpha_line)
    return pl.pallas_call(
        update,
        out_shape=(grid, line, grid, grid, line, grid),
        in_specs=[hbm] * len(sources),
        out_specs=[hbm] * 6,
        scratch_shapes=[
            *(pltpu.VMEM(source.shape, source.dtype) for source in sources),
            *(pltpu.VMEM(shape.shape, F32) for shape in (grid, line, grid, grid, line, grid)),
            pltpu.SemaphoreType.DMA((6, subs)),
            pltpu.SemaphoreType.DMA((5,)),
            pltpu.SemaphoreType.DMA((6, subs)),
        ],
        compiler_params=pltpu.CompilerParams(vmem_limit_bytes=60 * 1024 * 1024),
    )(*sources)


def solution(mesh):
    sizes = (mesh.shape["tm"], mesh.shape["gx"], mesh.shape["gy"])
    state, line = P("tm", None, "gx", "gy"), P("tm", "gx", "gy", None)
    return jax.shard_map(
        functools.partial(shards, sizes),
        mesh=mesh,
        in_specs=(state, line, state, state, line, state, line, state, state, line, P("tm")),
        out_specs=(state, line, state, state, line, state),
        check_vma=False,
    )
```

```python
import functools

import jax
import jax.numpy as jnp
from jax import lax
from jax.experimental import pallas as pl
from jax.experimental.pallas import tpu as pltpu
from jax.sharding import PartitionSpec as P

MAXSTEP = 4
DIFFUSION = 0.18
VERTICAL = 0.1
CENTRE = 1.0 - 4.0 * DIFFUSION - 2.0 * VERTICAL
FORWARD, ADJOINT = 0, 1
LOW, HIGH, SIDE = 0, 1, 2
PAD = 8
MESH = pl.DeviceIdType.MESH
F32, BF16 = jnp.float32, jnp.bfloat16


def pieces(value):
    high = value.astype(BF16)
    rest = value - high.astype(F32)
    mid = rest.astype(BF16)
    low = (rest - mid.astype(F32)).astype(BF16)
    return high, mid, low


def kernel(
    sizes,
    lagr_in, obs_lagr_in, incr_in, forcing_in, depart_in, model_var_in, obs_var_in, wind_e_in, wind_n_in,
    cells_in, counts,
    res_m, res_o, res_v, img_m, img_o, img_v, alpha_grid, alpha_line,
    lagr, obs_lagr, incr, forcing, depart, model_var, obs_var, wind_e, wind_n, cells, load_sem,
    field_00, field_01, field_10, field_11, half_e, half_n, from_west, from_east, later, onehot, spread_buf, next_lagr, next_model, next_image, arrived,
    last_image, leaving, row_out, row_in, col_out, col_in, part_out, part_in,
    send_sem, recv_sem, wide_send, wide_recv, part_send, part_recv,
):
    n_tm, n_gx, n_gy = sizes
    subs, levels, rows, lanes = incr.shape
    flat = levels * rows
    end = subs - 1
    field = ((field_00, field_01), (field_10, field_11))
    inner = pl.ds(PAD, rows)
    before = pl.ds(PAD - 1, rows)
    after = pl.ds(PAD + 1, rows)
    tm, gx, gy = lax.axis_index("tm"), lax.axis_index("gx"), lax.axis_index("gy")
    lane = lax.broadcasted_iota(jnp.int32, (rows, lanes), 1)
    out_edge = jnp.where(gy == 0, lanes - 1, 0)
    sign = jnp.where(gy == 0, -1.0, 1.0)
    at_edge = lane == out_edge
    at_first, at_last = lane == 0, lane == lanes - 1

    loads = [
        pltpu.make_async_copy(src, dst, load_sem.at[at])
        for at, (src, dst) in enumerate((
            (incr_in, incr), (lagr_in, lagr), (wind_e_in, wind_e), (wind_n_in, wind_n),
            (cells_in, cells), (model_var_in, model_var), (forcing_in, forcing),
            (obs_lagr_in, obs_lagr), (obs_var_in, obs_var), (depart_in, depart),
        ))
    ]
    for load in loads:
        load.start()

    row_in[...] = jnp.zeros_like(row_in)
    next_lagr[...] = jnp.zeros_like(next_lagr)
    next_model[...] = jnp.zeros_like(next_model)
    next_image[...] = jnp.zeros_like(next_image)
    arrived[...] = jnp.zeros_like(arrived)
    last_image[...] = jnp.zeros_like(last_image)

    plane = [
        {"gx": lax.rem(gx + a, n_gx), "gy": lax.rem(gy + b, n_gy)}
        for a in range(n_gx) for b in range(n_gy) if a + b > 0
    ]
    column_peers = [{"tm": lax.rem(tm + k, n_tm)} for k in range(1, n_tm)]
    barrier = pltpu.get_barrier_semaphore()
    for peer in plane + column_peers:
        pl.semaphore_signal(barrier, inc=1, device_id=peer, device_id_type=MESH)

    def wide(index, src, dst, step):
        return pltpu.make_async_remote_copy(
            src_ref=src, dst_ref=dst, send_sem=wide_send.at[index], recv_sem=wide_recv.at[index],
            device_id={"tm": lax.rem(tm + step + n_tm, n_tm)}, device_id_type=MESH,
        )

    sent_lagr = wide(0, lagr.at[0], next_lagr, -1)
    sent_model = wide(1, img_m.at[0], next_model, -1)
    sent_forward = wide(2, leaving, arrived, 1)
    sent_image = wide(3, img_m.at[0], next_image, -1)
    sent_last = wide(4, field_10.at[end, pl.ds(1, levels), inner], last_image, 1)
    not_first, not_last = tm > 0, tm < n_tm - 1

    def sends(kind, turn):
        pairs = []
        for side, axis, to, allowed in (
            (LOW, "gx", lax.rem(gx + n_gx - 1, n_gx), gx > 0),
            (HIGH, "gx", lax.rem(gx + 1, n_gx), gx < n_gx - 1),
            (SIDE, "gy", lax.rem(gy + 1, n_gy), None),
        ):
            if side == SIDE:
                src, dst, back = col_out.at[kind, turn], col_in.at[kind, turn], None
            else:
                src, dst = row_out.at[kind, turn, side], row_in.at[kind, turn, 1 - side]
                back = gx < n_gx - 1 if side == LOW else gx > 0
            arrival = SIDE if side == SIDE else 1 - side
            copy = pltpu.make_async_remote_copy(
                src_ref=src, dst_ref=dst,
                send_sem=send_sem.at[kind, turn, side], recv_sem=recv_sem.at[kind, turn, arrival],
                device_id={axis: to}, device_id_type=MESH,
            )
            pairs.append((copy, allowed, back))
        return pairs

    def guarded(condition, action):
        if condition is None:
            action()
        else:
            pl.when(condition)(action)

    def start_halo(kind, turn):
        for copy, allowed, _ in sends(kind, turn):
            guarded(allowed, copy.start)

    def wait_halo(kind, turn):
        for copy, _, back in sends(kind, turn):
            guarded(back, copy.wait_recv)

    def put(kind, turn, target, s, level, new, packed):
        target[s, level + 1, inner] = new
        first, last = new[0:1], new[rows - 1 : rows]
        edge = new
        if kind == ADJOINT:
            first = (DIFFUSION + half_e[s, level, PAD : PAD + 1]) * first
            last = (DIFFUSION - half_e[s, level, PAD + rows - 1 : PAD + rows]) * last
            edge = (DIFFUSION + sign * half_n[s, level]) * new
        row_out[kind, turn, LOW, s, pl.ds(level, 1)] = first
        row_out[kind, turn, HIGH, s, pl.ds(level, 1)] = last
        at = s * levels + level
        moved = pltpu.roll(edge, lax.rem(at - out_edge + lanes, lanes), 1)
        return jnp.where(lane == at, moved, packed)

    def over_levels(visit):
        group = 4
        turns_of = levels // group

        def body(at, packed):
            s, first = lax.div(at, turns_of), lax.rem(at, turns_of) * group
            for k in range(group):
                packed = visit(s, first + k, packed)
            return packed

        return lax.fori_loop(0, subs * turns_of, body, jnp.zeros((rows, lanes), F32))

    def begin(kind, turn, source):
        def visit(s, level, packed):
            return put(kind, turn, field[kind ^ (turn // MAXSTEP)][0], s, level, source[s, level], packed)

        col_out[kind, turn] = over_levels(visit)

    def step(kind, operator, j):
        turn = operator * MAXSTEP + j
        wait_halo(kind, turn)
        following = turn + 1 if j < MAXSTEP - 1 else 2 * MAXSTEP
        source, target = (field[kind ^ operator][(j + at) % 2] for at in range(2))

        def visit(s, level, packed):
            source[s, level + 1, PAD - 1 : PAD] = row_in[kind, turn, LOW, s, pl.ds(level, 1)]
            source[s, level + 1, PAD + rows : PAD + rows + 1] = row_in[kind, turn, HIGH, s, pl.ds(level, 1)]
            running = jnp.broadcast_to(counts[s], (rows, lanes)) > j
            at = s * levels + level
            here = source[s, level + 1, inner]
            east = source[s, level + 1, after]
            west = source[s, level + 1, before]
            column = pltpu.roll(col_in[kind, turn], lax.rem(out_edge - at + lanes, lanes), 1)
            column = jnp.where(at_edge, column, 0.0)
            level_sum = source[s, level + 2, inner] + source[s, level, inner]
            wind = half_n[s, level]
            if kind == FORWARD:
                north = jnp.where(at_last, column, pltpu.roll(here, lanes - 1, 1))
                south = jnp.where(at_first, column, pltpu.roll(here, 1, 1))
                stepped = (
                    CENTRE * here
                    + DIFFUSION * ((east + west) + (north + south))
                    + half_e[s, level, inner] * (west - east)
                    + wind * (south - north)
                    + VERTICAL * level_sum
                )
            else:
                north = pltpu.roll((DIFFUSION + wind) * here, lanes - 1, 1)
                south = pltpu.roll((DIFFUSION - wind) * here, 1, 1)
                stepped = (
                    CENTRE * here
                    + from_west[s, level] * west
                    + from_east[s, level] * east
                    + jnp.where(at_first, column, south)
                    + jnp.where(at_last, column, north)
                    + VERTICAL * level_sum
                )
            new = jnp.where(running, stepped, here)
            return put(kind, following, target, s, level, new, packed)

        packed = over_levels(visit)

        if j < MAXSTEP - 1:
            col_out[kind, following] = packed
            start_halo(kind, following)

    def where_lane(s):
        return lax.broadcasted_iota(jnp.int32, (lanes, cells.shape[3]), 0) == lax.rem(cells[s, 0], lanes)

    def observe(s, value):
        turned = value.reshape(flat, lanes).T
        parts = jnp.concatenate(pieces(turned), 0)
        picked = jnp.dot(parts, onehot[s], preferred_element_type=F32)
        whole = (picked[:lanes] + picked[lanes : 2 * lanes]) + picked[2 * lanes :]
        return jnp.sum(jnp.where(where_lane(s), whole, 0.0), 0, keepdims=True)

    def spread(s, value):
        mask = where_lane(s)
        parts = jnp.concatenate(
            [jnp.where(mask, part.astype(F32), 0.0).astype(BF16) for part in pieces(value)], 0
        )
        summed = lax.dot_general(
            onehot[s], parts, (((1,), (1,)), ((), ())), preferred_element_type=F32
        )
        whole = (summed[:, :lanes] + summed[:, lanes : 2 * lanes]) + summed[:, 2 * lanes :]
        return whole.reshape(levels, rows, lanes)

    for kind in (FORWARD, ADJOINT):
        for slot in range(2):
            for s in range(subs):
                for edge in (0, levels + 1):
                    field[kind][slot][s, edge] = jnp.zeros(field_00.shape[2:], F32)
    loads[0].wait()
    begin(FORWARD, 0, incr)
    loads[1].wait()
    pl.semaphore_wait(barrier, len(plane) + len(column_peers))

    @pl.when(not_first)
    def _():
        sent_lagr.start()

    start_halo(FORWARD, 0)
    loads[5].wait()
    loads[6].wait()
    for s in range(subs):
        img_m[s] = forcing[s] - model_var[s] * lagr[s] - incr[s]

    loads[2].wait()
    loads[3].wait()
    half_e[...] = jnp.zeros_like(half_e)
    for s in range(subs):
        half_n[s] = 0.5 * wind_n[s]
        half_e[s, :, inner] = 0.5 * wind_e[s]
        half_e[s, :, PAD - 1 : PAD] = jnp.full((levels, 1, lanes), DIFFUSION - 1.0, F32)
        half_e[s, :, PAD + rows : PAD + rows + 1] = jnp.full((levels, 1, lanes), 1.0 - DIFFUSION, F32)
    for s in range(subs):
        from_west[s] = DIFFUSION - half_e[s, :, before]
        from_east[s] = DIFFUSION + half_e[s, :, after]
    loads[4].wait()
    for s in range(subs):
        chosen = lax.div(cells[s, 0], lanes)
        place = lax.broadcasted_iota(jnp.int32, (flat, cells.shape[3]), 0)
        onehot[s] = jnp.where(place == chosen, 1.0, 0.0).astype(BF16)
    for load in loads[7:]:
        load.wait()

    def first_spread(s):
        spread_buf[s] = spread(s, obs_lagr[s, 0])

    def first_observe(s):
        res_o[s, 0] = depart[s, 0] - (obs_var[s, 0] * obs_lagr[s, 0] + observe(s, incr[s]))

    def second_spread(s):
        spread_buf[s] = spread(s, res_o[s, 0])

    def second_observe(s):
        img_o[s, 0] = obs_var[s, 0] * res_o[s, 0] + observe(s, res_v[s])

    step(FORWARD, 0, 0)

    @pl.when(not_last)
    def _():
        sent_lagr.wait_recv()

    for s in range(end):
        later[s] = lagr[s + 1]
    later[end] = next_lagr[...]
    begin(ADJOINT, 0, later)
    start_halo(ADJOINT, 0)

    @pl.when(not_first)
    def _():
        sent_model.start()

    for s in range(end):
        first_spread(s)
    step(FORWARD, 0, 1)
    first_spread(end)
    step(ADJOINT, 0, 0)
    for s in range(end):
        first_observe(s)
    step(FORWARD, 0, 2)
    first_observe(end)
    step(ADJOINT, 0, 1)
    step(FORWARD, 0, 3)
    forward = field[FORWARD][0]
    leaving[...] = forward[end, pl.ds(1, levels), inner]

    @pl.when(not_last)
    def _():
        sent_forward.start()

    step(ADJOINT, 0, 2)

    @pl.when(not_last)
    def _():
        sent_model.wait_recv()

    live = jnp.where(not_last, 1.0, 0.0)
    for s in range(1, subs):
        res_m[s] = img_m[s] + forward[s - 1, pl.ds(1, levels), inner]
    next_model[...] = live * (next_model[...] + leaving[...])
    for s in range(end):
        later[s] = res_m[s + 1]
    later[end] = next_model[...]
    begin(ADJOINT, MAXSTEP, later)
    start_halo(ADJOINT, MAXSTEP)
    step(ADJOINT, 0, 3)
    for s in range(subs):
        res_v[s] = field[ADJOINT][0][s, pl.ds(1, levels), inner] - lagr[s] - spread_buf[s]
    begin(FORWARD, MAXSTEP, res_v)
    start_halo(FORWARD, MAXSTEP)
    step(ADJOINT, 1, 0)
    for s in range(end):
        second_spread(s)
    step(FORWARD, 1, 0)
    second_spread(end)

    @pl.when(not_first)
    def _():
        sent_model.wait_send()
        sent_forward.wait_recv()

    res_m[0] = img_m[0] + arrived[...]
    for s in range(subs):
        img_m[s] = model_var[s] * res_m[s] + res_v[s]

    @pl.when(not_first)
    def _():
        sent_image.start()

    step(ADJOINT, 1, 1)
    for s in range(end):
        second_observe(s)
    step(FORWARD, 1, 1)
    second_observe(end)
    step(ADJOINT, 1, 2)
    step(FORWARD, 1, 2)
    step(ADJOINT, 1, 3)
    step(FORWARD, 1, 3)

    @pl.when(not_last)
    def _():
        sent_last.start()
        sent_image.wait_recv()

    cross = jnp.zeros((rows, lanes), F32)
    square = jnp.zeros((rows, lanes), F32)
    for s in range(subs):
        for level in range(levels):
            image = res_m[s, level] - field[FORWARD][0][s, level + 1, inner] + spread_buf[s, level]
            img_v[s, level] = image
            cross = cross + res_v[s, level] * image
            square = square + image * image
    for s in range(1, subs):
        for level in range(levels):
            image = img_m[s, level] - field[ADJOINT][0][s - 1, level + 1, inner]
            img_m[s, level] = image
            cross = cross + res_m[s, level] * image
            square = square + image * image
    alone = jnp.where(not_first, 0.0, 1.0)
    for level in range(levels):
        image = live * (next_image[level] - field[ADJOINT][0][end, level + 1, inner])
        cross = cross + next_model[level] * image
        square = square + image * image
        image = alone * img_m[0, level]
        cross = cross + res_m[0, level] * image
        square = square + image * image
    obs_cross = jnp.zeros((1, cells.shape[3]), F32)
    obs_square = jnp.zeros((1, cells.shape[3]), F32)
    for s in range(subs):
        obs_cross = obs_cross + res_o[s, 0] * img_o[s, 0]
        obs_square = obs_square + img_o[s, 0] * img_o[s, 0]

    def folded(grid, line):
        tile = jnp.sum(grid.reshape(rows // 8, 8, lanes), 0)
        for at in range(0, line.shape[1], lanes):
            piece = line[:, at : at + lanes]
            head = lax.broadcasted_iota(jnp.int32, (8, lanes), 0) == 0
            tile = tile + jnp.where(head, jnp.broadcast_to(piece, (8, lanes)), 0.0)
        return tile

    both = jnp.concatenate([folded(cross, obs_cross), folded(square, obs_square)], 0)
    base = 0
    for phase, targets in enumerate((plane, column_peers)):
        part_out[phase] = both
        copies = []
        for target in targets:
            copy = pltpu.make_async_remote_copy(
                src_ref=part_out.at[phase], dst_ref=part_in.at[base],
                send_sem=part_send.at[base], recv_sem=part_recv.at[base],
                device_id=target, device_id_type=MESH,
            )
            copy.start()
            copies.append((copy, base))
            base += 1
        for copy, slot in copies:
            copy.wait_recv()
            both = both + part_in[slot]
        for copy, _ in copies:
            copy.wait_send()
    total_cross = jnp.sum(jnp.sum(both[:8], 0, keepdims=True), 1, keepdims=True)
    total_square = jnp.sum(jnp.sum(both[8:], 0, keepdims=True), 1, keepdims=True)
    alpha = total_cross / (total_square + 1e-06)
    alpha_grid[0, 0] = jnp.broadcast_to(alpha, alpha_grid.shape[2:])
    alpha_line[0, 0] = jnp.broadcast_to(alpha, alpha_line.shape[2:])

    @pl.when(not_first)
    def _():
        sent_last.wait_recv()
        sent_lagr.wait_send()
        sent_image.wait_send()

    img_m[0] = img_m[0] - last_image[...]

    @pl.when(not_last)
    def _():
        sent_forward.wait_send()
        sent_last.wait_send()

    def drain(turn, carry):
        for kind in (FORWARD, ADJOINT):
            for copy, allowed, _ in sends(kind, turn):
                guarded(allowed, copy.wait_send)
        return carry

    lax.fori_loop(0, 2 * MAXSTEP, drain, 0)


def update(*refs):
    sources, targets, held, made = refs[:11], refs[11:17], refs[17:28], refs[28:34]
    load_sem, small_sem, store_sem = refs[34:]
    subs = held[0].shape[0]
    small = [pltpu.make_async_copy(sources[6 + at], held[6 + at], small_sem.at[at]) for at in range(5)]
    loads = [
        [pltpu.make_async_copy(sources[at].at[s], held[at].at[s], load_sem.at[at, s]) for at in range(6)]
        for s in range(subs)
    ]
    stores = [
        [pltpu.make_async_copy(made[at].at[s], targets[at].at[s], store_sem.at[at, s]) for at in range(6)]
        for s in range(subs)
    ]
    small[3].start()
    for group in loads:
        for load in group:
            load.start()
    for at in (0, 1, 2, 4):
        small[at].start()
    lagr, incr, res_m, res_v, img_m, img_v, obs_lagr, res_o, img_o, alpha_grid, alpha_line = held
    small[3].wait()
    alpha = alpha_grid[0]
    for s in range(subs):
        for load in loads[s]:
            load.wait()
        made[0][s] = lagr[s] + alpha * res_m[s]
        stores[s][0].start()
        made[2][s] = incr[s] + alpha * res_v[s]
        stores[s][2].start()
        made[3][s] = res_m[s] - alpha * img_m[s]
        stores[s][3].start()
        made[5][s] = res_v[s] - alpha * img_v[s]
        stores[s][5].start()
    for at in (0, 1, 2, 4):
        small[at].wait()
    for s in range(subs):
        made[1][s] = obs_lagr[s] + alpha_line[0] * res_o[s]
        stores[s][1].start()
        made[4][s] = res_o[s] - alpha_line[0] * img_o[s]
        stores[s][4].start()
    for group in stores:
        for store in group:
            store.wait()


def shards(sizes, *operands):
    lagrange, obs_lagrange, increment = operands[:3]
    subs, levels, rows, lanes = increment.shape
    nobs = obs_lagrange.shape[3]
    n_tm, n_gx, n_gy = sizes
    grid = jax.ShapeDtypeStruct(increment.shape, F32)
    line = jax.ShapeDtypeStruct(obs_lagrange.shape, F32)
    state = pltpu.VMEM((levels, rows, lanes), F32)
    turns = 2 * MAXSTEP
    partners = n_gx * n_gy - 1 + n_tm - 1
    vmem = pl.BlockSpec(memory_space=pltpu.VMEM)
    hbm = pl.BlockSpec(memory_space=pltpu.HBM)
    res_m, res_o, res_v, img_m, img_o, img_v, alpha, alpha_line = pl.pallas_call(
        functools.partial(kernel, sizes),
        out_shape=(grid, line, grid, grid, line, grid, jax.ShapeDtypeStruct((1, 1, 1, lanes), F32),
                   jax.ShapeDtypeStruct((1, 1, 1, nobs), F32)),
        in_specs=[hbm] * 10 + [pl.BlockSpec(memory_space=pltpu.SMEM)],
        out_specs=[vmem] * 8,
        scratch_shapes=[
            *(pltpu.VMEM(operand.shape, operand.dtype) for operand in operands[:10]),
            pltpu.SemaphoreType.DMA((10,)),
            *[pltpu.VMEM((subs, levels + 2, rows + 2 * PAD, lanes), F32)] * 4,
            pltpu.VMEM((subs, levels, rows + 2 * PAD, lanes), F32),
            *[pltpu.VMEM((subs, levels, rows, lanes), F32)] * 4,
            pltpu.VMEM((subs, levels * rows, nobs), BF16),
            pltpu.VMEM((subs, levels, rows, lanes), F32),
            state, state, state, state, state, state,
            pltpu.VMEM((2, turns + 1, 2, subs, levels, lanes), F32),
            pltpu.VMEM((2, turns, 2, subs, levels, lanes), F32),
            pltpu.VMEM((2, turns, rows, lanes), F32),
            pltpu.VMEM((2, turns, rows, lanes), F32),
            pltpu.VMEM((2, 16, lanes), F32),
            pltpu.VMEM((partners, 16, lanes), F32),
            pltpu.SemaphoreType.DMA((2, turns, 3)),
            pltpu.SemaphoreType.DMA((2, turns, 3)),
            pltpu.SemaphoreType.DMA((5,)),
            pltpu.SemaphoreType.DMA((5,)),
            pltpu.SemaphoreType.DMA((partners,)),
            pltpu.SemaphoreType.DMA((partners,)),
        ],
        compiler_params=pltpu.CompilerParams(
            collective_id=0, has_side_effects=True, vmem_limit_bytes=60 * 1024 * 1024
        ),
    )(*operands)
    sources = (lagrange, increment, res_m, res_v, img_m, img_v, obs_lagrange, res_o, img_o, alpha, alpha_line)
    return pl.pallas_call(
        update,
        out_shape=(grid, line, grid, grid, line, grid),
        in_specs=[hbm] * len(sources),
        out_specs=[hbm] * 6,
        scratch_shapes=[
            *(pltpu.VMEM(source.shape, source.dtype) for source in sources),
            *(pltpu.VMEM(shape.shape, F32) for shape in (grid, line, grid, grid, line, grid)),
            pltpu.SemaphoreType.DMA((6, subs)),
            pltpu.SemaphoreType.DMA((5,)),
            pltpu.SemaphoreType.DMA((6, subs)),
        ],
        compiler_params=pltpu.CompilerParams(vmem_limit_bytes=60 * 1024 * 1024),
    )(*sources)


def solution(mesh):
    sizes = (mesh.shape["tm"], mesh.shape["gx"], mesh.shape["gy"])
    state, line = P("tm", None, "gx", "gy"), P("tm", "gx", "gy", None)
    return jax.shard_map(
        functools.partial(shards, sizes),
        mesh=mesh,
        in_specs=(state, line, state, state, line, state, line, state, state, line, P("tm")),
        out_specs=(state, line, state, state, line, state),
        check_vma=False,
    )
```
